128 devices in a mesh: row: 16 (over z, y), col: 8 (over x, core).
Axes of the slice: x: 4, y: 4, z: 4, core: 2. Of those that a mesh axis runs over, the one named last changes fastest.
Arguments:
- rhs: float32 [1, 128, 256, 4096], P(None, ('row', 'col')), may hold values from -6 to 6
- panel: bfloat16 [1, 128, 256, 1024], P(None, ('row', 'col')), may hold values from -0.375 to 0.375
- diag_inverse: float32 [4, 256, 256], replicated, may hold values from -1 to 1.5, as said below
Outputs:
- solution: float32 [1024, 4096], replicated
- trailing: float32 [1, 128, 256, 4096], P(None, ('row', 'col'))
The draws below stay inside these ranges and needn't reach their ends.
Inputs may be any that keep to these rules, and one draw needn't show every extreme that they name: `diag_inverse`: each of the 4 blocks is lower triangular with diagonal entries between 0.5 and 1.5.
All inputs are finite; a program needn't handle non-finite values.
Results may differ from the reference program's by a relative error of at most 0.0043.
Values may be sent and summed in bfloat16 or wider, within the bound.
A program may use at most 192 MiB of HBM per device.

```python
import math
import jax
import jax.numpy as jnp
from jax import lax

NB = 256
STEPS = 4
S = 4096
K = 1024
LB = 1
N_ROW = 16
N_COL = 8


def draw_diag_inverse(key, part):
    key = jax.random.fold_in(key, 7)
    first, second = jax.random.split(key)
    rows = jnp.arange(NB)[:, None]
    cols = jnp.arange(NB)[None, :]
    spread = jax.random.normal(first, (STEPS, NB, NB), jnp.float32)
    lower = jnp.where(rows > cols, spread * (0.5 / math.sqrt(NB)), 0.0)
    lower = jnp.clip(lower, -0.9, 0.9)
    diagonal = jax.random.uniform(second, (STEPS, NB), jnp.float32, 0.5, 1.5)
    return lower + diagonal[:, :, None] * jnp.eye(NB, dtype=jnp.float32)[None, :, :]


def block_levels(own_key, shape, shards, low, high):
    def one(dim, shards_of):
        heights = jax.random.uniform(jax.random.fold_in(jax.random.fold_in(own_key, 6), dim), (shards_of,), jnp.float32, low / len(shards), high / len(shards))
        return jnp.repeat(jnp.exp(heights), shape[dim] // shards_of).reshape((-1,) + (1,) * (len(shape) - dim - 1))

    factor_of = one(*shards[0])
    for cut in shards[1:]:
        factor_of = factor_of * one(*cut)
    return factor_of


def scatter_about(key, extent, scale, bound, cuts=(), kind=jnp.bfloat16):
    drawn = jax.random.normal(key, extent, jnp.float32) * scale
    if len(cuts) > 0:
        drawn = block_levels(key, extent, cuts, -0.22, 0.18) * drawn
    return jnp.clip(drawn, min=-bound, max=bound).astype(kind)


def setup_inputs(seed: int = 0) -> dict:
    key_list = jax.random.split(jax.random.key(seed), 4)
    rhs = scatter_about(key_list[0], (LB, N_ROW * N_COL, NB, S), 1.0, 6.0, ((1, 128),), jnp.float32)
    panel = scatter_about(key_list[1], (LB, N_ROW * N_COL, NB, K), NB ** -0.5, 0.375, ((1, 128),))
    diag_inverse = draw_diag_inverse(jax.random.fold_in(key_list[3], 71), 0)
    return dict(rhs=rhs, panel=panel, diag_inverse=diag_inverse)


def reference(rhs, panel, diag_inverse):
    blocks_all = rhs.shape[0] * rhs.shape[1]
    width = rhs.shape[2]
    shots = rhs.shape[3]
    work = rhs.reshape(blocks_all, width, shots)
    factor = panel.reshape(blocks_all, width, panel.shape[3])
    numbers = jnp.arange(blocks_all, dtype=jnp.int32)
    solved_list = []
    for step in range(diag_inverse.shape[0]):
        solved = jnp.dot(diag_inverse[step], work[step], precision=lax.Precision.HIGHEST, preferred_element_type=jnp.float32)
        solved_list.append(solved)
        solved_low = solved.astype(jnp.bfloat16)
        columns = factor[:, :, step * width:(step + 1) * width].reshape(blocks_all * width, width)
        update = jnp.dot(columns, solved_low, preferred_element_type=jnp.float32).reshape(blocks_all, width, shots)
        below = (numbers > step)[:, None, None]
        work = work - jnp.where(below, update, jnp.zeros_like(update))
    solution = jnp.concatenate(solved_list, axis=0)
    return solution, work.reshape(rhs.shape)
```

```python
import jax
import jax.numpy as jnp
from jax import lax
from jax.experimental import pallas as pl
from jax.experimental.pallas import tpu as pltpu
from jax.sharding import PartitionSpec as P

MESH = pl.DeviceIdType.MESH
NB = 256
TW = 128
TILES = 32
PER = 8
CHUNKS = TILES // PER
ROOTS = 2
LAG = 4
KINDS = (("y", 1), ("z", 1), ("x", 0), ("y", 3), ("z", 3), ("x", 1), ("y", 2), ("z", 2))
PLANE = {"x": ("z", "y"), "y": ("z", "x"), "z": ("y", "x")}


def place():
    row, col = lax.axis_index("row"), lax.axis_index("col")
    return {"z": row // 4, "y": row % 4, "x": col // 2}, col % 2


def device(at, core):
    return (at["z"] * 4 + at["y"], at["x"] * 2 + core)


def moved(at, axis, by):
    new = dict(at)
    new[axis] = (at[axis] + by) % 4
    return new


def spread_kernel(
    rhs, panel, dinv, buf, rhs_v, panel_v, dinv_v, local, got, sent_b, sent_c, sent_a, sent_core
):
    at, core = place()
    me = lax.axis_index("row") * 8 + lax.axis_index("col")

    def send(block, tile, sem, to):
        pltpu.make_async_remote_copy(
            src_ref=buf.at[block, tile],
            dst_ref=buf.at[block, tile],
            send_sem=sem,
            recv_sem=got.at[block, tile],
            device_id=to,
            device_id_type=MESH,
        ).start()

    def take(block, tile):
        ref = buf.at[block, tile]
        pltpu.make_async_copy(ref, ref, got.at[block, tile]).wait()

    def drain(sem, count):
        ref = buf.at[0, pl.ds(0, count)]
        pltpu.make_async_copy(ref, ref, sem).wait()

    def rhs_copy(chunk):
        cols = pl.ds(pl.multiple_of(chunk * PER * TW, PER * TW), PER * TW)
        return pltpu.make_async_copy(rhs.at[:, cols], rhs_v.at[:, cols], local.at[chunk])

    panel_copy = pltpu.make_async_copy(panel, panel_v, local.at[CHUNKS])

    def dinv_copy(block):
        return pltpu.make_async_copy(dinv.at[block], dinv_v, local.at[CHUNKS + 1])

    peers = [(moved(at, axis, by), core) for axis in "xyz" for by in (1, 2, 3)]
    peers.append((at, 1 - core))
    barrier = pltpu.get_barrier_semaphore()
    for where, which in peers:
        pl.semaphore_signal(barrier, inc=1, device_id=device(where, which), device_id_type=MESH)

    @pl.when(me < 4)
    def _():
        dinv_copy(me).start()
        rhs_copy(0).start()
        panel_copy.start()
        for chunk in range(1, CHUNKS):
            rhs_copy(chunk).start()

    pl.semaphore_wait(barrier, len(peers))

    def kind(index, root):
        axis, j = KINDS[index]
        if axis == "x":
            j = 2 - root + j
        return axis, j

    def solve(owner, chunk):
        root = owner // 2
        rhs_copy(chunk).wait()

        @pl.when(chunk == 0)
        def _():
            dinv_copy(owner).wait()
            panel_copy.wait()

        for pair in range(PER // 2):
            tile = chunk * PER + 2 * pair
            for before in range(owner):
                if owner == 2 and before == 0 or owner == 3 and before == 1:
                    continue
                take(before, tile)
                take(before, tile + 1)
            cols = pl.ds(pl.multiple_of(tile * TW, 2 * TW), 2 * TW)
            work = rhs_v[:, cols]
            for before in range(owner):
                low = jnp.concatenate([buf[before, tile], buf[before, tile + 1]], axis=1)
                work = work - jnp.dot(
                    panel_v[:, before * NB : (before + 1) * NB], low, preferred_element_type=jnp.float32
                )
            solved = jnp.dot(
                dinv_v[...], work, precision=lax.Precision.HIGHEST, preferred_element_type=jnp.float32
            ).astype(jnp.bfloat16)
            for half in range(2):
                buf[owner, tile + half] = solved[:, half * TW : (half + 1) * TW]
                axis, j = kind(2 * pair + half, root)
                send(owner, tile + half, sent_b.at[root, tile + half], device(moved(at, axis, j), core))
                send(owner, tile + half, sent_core.at[root, tile + half], device(at, 1 - core))

    def roles(index, root):
        axis, j = kind(index, root)
        one, two = PLANE[axis]
        rel = {"x": (at["x"] - root + 4) % 4, "y": at["y"], "z": at["z"]}
        a, b, c = rel[axis], rel[one], rel[two]
        line = (a == j) & (b == 0) & (c == 0)
        root_here = (a == 0) & (b == 0) & (c == 0)
        edge = (a == j) & (b != 0) & (c == 0)
        inner = (a == j) & (c != 0)
        stage = jnp.where(line, 0, jnp.where(edge, 1, jnp.where(inner, 2, jnp.where(root_here, -1, 3))))
        return axis, one, two, a, stage

    def handle(index, root, chunk, stage):
        axis, one, two, a, mine = roles(index, root)
        block = 2 * root + core
        tile = chunk * PER + index

        @pl.when(mine == stage)
        def _():
            take(block, tile)

            @pl.when(mine == 0)
            def _():
                for by in (1, 3, 2):
                    send(block, tile, sent_b.at[root, tile], device(moved(at, one, by), core))

            @pl.when(mine <= 1)
            def _():
                for by in (1, 3, 2):
                    send(block, tile, sent_c.at[root, tile], device(moved(at, two, by), core))

            @pl.when(mine <= 2)
            def _():
                for by in (1, 3, 2):

                    @pl.when((mine != 0) | ((a + by) % 4 != 0))
                    def _():
                        send(block, tile, sent_a.at[root, tile], device(moved(at, axis, by), core))

            send(block, tile, sent_core.at[root, tile], device(at, 1 - core))

    def step(t, _):
        for owner in (0, 1):

            @pl.when((me == owner) & (t < CHUNKS))
            def _():
                solve(owner, t)

        def sub(stage, _):
            g = t - stage

            @pl.when((g >= 0) & (g < ROOTS * CHUNKS))
            def _():
                for index in range(PER):
                    handle(index, g // CHUNKS, g % CHUNKS, stage)

            return 0

        lax.fori_loop(0, 4, sub, 0)
        for owner in (2, 3):

            @pl.when((me == owner) & (t >= LAG - 1) & (t < LAG - 1 + CHUNKS))
            def _():
                solve(owner, t - (LAG - 1))

        return 0

    lax.fori_loop(0, ROOTS * CHUNKS + 3, step, 0)

    skip_first = (me == 1) | (me == 2) | (me == 3)

    def finish(tile, _):
        @pl.when(jnp.logical_not(skip_first))
        def _():
            take(1 - core, tile)

        @pl.when(me != 3)
        def _():
            take(3 - core, tile)

        return 0

    lax.fori_loop(0, TILES, finish, 0)

    def drain_all(chunk, _):
        for root in range(ROOTS):
            for index in range(PER):
                tile = chunk * PER + index
                _, _, _, _, mine = roles(index, root)
                drain(sent_core.at[root, tile], 1)

                @pl.when(mine == -1)
                def _():
                    drain(sent_b.at[root, tile], 1)

                @pl.when(mine == 0)
                def _():
                    drain(sent_b.at[root, tile], 3)
                    drain(sent_c.at[root, tile], 3)
                    drain(sent_a.at[root, tile], 2)

                @pl.when(mine == 1)
                def _():
                    drain(sent_c.at[root, tile], 3)
                    drain(sent_a.at[root, tile], 3)

                @pl.when(mine == 2)
                def _():
                    drain(sent_a.at[root, tile], 3)

        return 0

    lax.fori_loop(0, CHUNKS, drain_all, 0)


def spread(rhs, panel, dinv):
    any_space = pl.BlockSpec(memory_space=pl.ANY)
    rhs, panel, dinv = (pltpu.with_memory_space_constraint(array, pltpu.HBM) for array in (rhs, panel, dinv))
    sem = pltpu.SemaphoreType.DMA
    return pl.pallas_call(
        spread_kernel,
        out_shape=pltpu.VMEM((4, TILES, NB, TW), jnp.bfloat16),
        in_specs=[any_space] * 3,
        out_specs=pl.BlockSpec(memory_space=pltpu.VMEM),
        scratch_shapes=[
            pltpu.VMEM((NB, TILES * TW), jnp.float32),
            pltpu.VMEM((NB, 4 * NB), jnp.bfloat16),
            pltpu.VMEM((NB, NB), jnp.float32),
            sem((CHUNKS + 2,)),
            sem((4, TILES)),
            sem((ROOTS, TILES)),
            sem((ROOTS, TILES)),
            sem((ROOTS, TILES)),
            sem((ROOTS, TILES)),
        ],
        name="spread",
        compiler_params=pltpu.CompilerParams(
            collective_id=1, has_side_effects=True, vmem_limit_bytes=16 * 2**20
        ),
    )(rhs, panel, dinv)


GROUP = 4
WIDE = GROUP * TW
GROUPS = TILES // GROUP


def finish_kernel(buf, rhs, panel, sol, trail, stage, tstage, rhs_v, panel_v, load, out_s, out_t):
    me = lax.axis_index("row") * 8 + lax.axis_index("col")

    def rhs_copy(g):
        cols = pl.ds(g * WIDE, WIDE)
        return pltpu.make_async_copy(rhs.at[:, cols], rhs_v.at[:, cols], load.at[g])

    panel_copy = pltpu.make_async_copy(panel, panel_v, load.at[GROUPS])
    panel_copy.start()
    for g in range(GROUPS):
        rhs_copy(g).start()

    def sol_copy(g):
        return pltpu.make_async_copy(stage.at[g % 2], sol.at[:, pl.ds(g * WIDE, WIDE)], out_s.at[g % 2])

    def trail_copy(g):
        return pltpu.make_async_copy(tstage.at[g % 2], trail.at[:, pl.ds(g * WIDE, WIDE)], out_t.at[g % 2])

    for g in range(GROUPS):
        if g >= 2:
            sol_copy(g - 2).wait()
        for block in range(4):
            for i in range(GROUP):
                stage[g % 2, block * NB : (block + 1) * NB, i * TW : (i + 1) * TW] = buf[
                    block, g * GROUP + i
                ].astype(jnp.float32)
        sol_copy(g).start()
        if g == 0:
            panel_copy.wait()
            for block in range(4):
                cols = slice(block * NB, (block + 1) * NB)
                panel_v[:, cols] = jnp.where(me > block, panel_v[:, cols], jnp.zeros((NB, NB), jnp.bfloat16))
        rhs_copy(g).wait()
        if g >= 2:
            trail_copy(g - 2).wait()
        work = rhs_v[:, g * WIDE : (g + 1) * WIDE]
        for block in range(4):
            low = jnp.concatenate([buf[block, g * GROUP + i] for i in range(GROUP)], axis=1)
            work = work - jnp.dot(
                panel_v[:, block * NB : (block + 1) * NB], low, preferred_element_type=jnp.float32
            )
        tstage[g % 2] = work
        trail_copy(g).start()
    for g in (GROUPS - 2, GROUPS - 1):
        sol_copy(g).wait()
        trail_copy(g).wait()


def finish(buf, rhs, panel):
    any_space = pl.BlockSpec(memory_space=pl.ANY)
    buf = pltpu.with_memory_space_constraint(buf, pltpu.VMEM)
    return pl.pallas_call(
        finish_kernel,
        out_shape=(
            jax.ShapeDtypeStruct((4 * NB, TILES * TW), jnp.float32),
            jax.ShapeDtypeStruct((NB, TILES * TW), jnp.float32),
        ),
        in_specs=[pl.BlockSpec(memory_space=pltpu.VMEM), any_space, any_space],
        out_specs=(any_space, any_space),
        scratch_shapes=[
            pltpu.VMEM((2, 4 * NB, WIDE), jnp.float32),
            pltpu.VMEM((2, NB, WIDE), jnp.float32),
            pltpu.VMEM((NB, TILES * TW), jnp.float32),
            pltpu.VMEM((NB, 4 * NB), jnp.bfloat16),
            pltpu.SemaphoreType.DMA((GROUPS + 1,)),
            pltpu.SemaphoreType.DMA((2,)),
            pltpu.SemaphoreType.DMA((2,)),
        ],
        name="finish",
        compiler_params=pltpu.CompilerParams(vmem_limit_bytes=24 * 2**20),
    )(buf, rhs, panel)


def body(rhs, panel, diag_inverse):
    own = rhs.reshape(rhs.shape[2], rhs.shape[3])
    factor = panel.reshape(panel.shape[2], panel.shape[3])
    tiles = spread(own, factor, diag_inverse)
    solved, trailing = finish(tiles, own, factor)
    return solved, trailing.reshape(rhs.shape)


def solution(mesh):
    in_specs = (P(None, ("row", "col"), None, None), P(None, ("row", "col"), None, None), P())
    out_specs = (P(), P(None, ("row", "col"), None, None))
    return jax.shard_map(body, mesh=mesh, in_specs=in_specs, out_specs=out_specs, check_vma=False)
```

```python
import jax
import jax.numpy as jnp
from jax import lax
from jax.experimental import pallas as pl
from jax.experimental.pallas import tpu as pltpu
from jax.sharding import PartitionSpec as P

MESH = pl.DeviceIdType.MESH
NB = 256
TW = 128
TILES = 32
PER = 8
SIDE = PER // 2
CHUNKS = TILES // PER
ROOTS = 2
WIDTH = SIDE * TW
PIECES = 2
ROWS = NB // PIECES
UNITS = CHUNKS * PIECES
STRIDE = 2
LATE = 8
KINDS = (("y", 1), ("z", 1), ("x", 0), ("y", 3), ("z", 3), ("x", 1), ("y", 2), ("z", 2))
PLANE = {"x": ("z", "y"), "y": ("x", "z"), "z": ("y", "x")}


def place():
    row, col = lax.axis_index("row"), lax.axis_index("col")
    return {"z": row // 4, "y": row % 4, "x": col // 2}, col % 2


def device(at, core):
    return (at["z"] * 4 + at["y"], at["x"] * 2 + core)


def moved(at, axis, by):
    new = dict(at)
    new[axis] = (at[axis] + by) % 4
    return new


def split(value):
    first = value.astype(jnp.bfloat16)
    rest = value - first.astype(jnp.float32)
    second = rest.astype(jnp.bfloat16)
    third = (rest - second.astype(jnp.float32)).astype(jnp.bfloat16)
    return first, second, third


def dot(left, right):
    return jnp.dot(left, right, preferred_element_type=jnp.float32)


def spread_kernel(
    rhs, panel, dinv, buf, rhs_v, panel_v, dinv_v, parts, local, swap_out, swap_in, got, core_in, core_out, sent
):
    at, core = place()
    me = lax.axis_index("row") * 8 + lax.axis_index("col")
    sibling = device(at, 1 - core)
    first_root, second_root = me // 2 == 0, me // 2 == 1

    def spot(root, chunk, index):
        block = jnp.where(root == 0, core, 2 + index // SIDE)
        tile = chunk * PER + jnp.where(root == 0, index, core * SIDE + index % SIDE)
        return block, tile

    def send(block, tile, h, send_sem, recv_sem, to):
        piece = buf.at[block, tile, pl.ds(pl.multiple_of(h * ROWS, ROWS), ROWS)]
        pltpu.make_async_remote_copy(
            src_ref=piece,
            dst_ref=piece,
            send_sem=send_sem,
            recv_sem=recv_sem,
            device_id=to,
            device_id_type=MESH,
        ).start()

    def wait(ref, sem):
        pltpu.make_async_copy(ref, ref, sem).wait()

    def wait_tiles(count, sem):
        wait(buf.at[pl.ds(0, 2), pl.ds(0, count // 2)], sem)

    def take(root, chunk, index, h):
        wait(buf.at[0, 0, pl.ds(0, ROWS)], got.at[root, chunk * PER + index, h])

    def pass_over(root, chunk, index, h):
        block, tile = spot(root, chunk, index)
        send(block, tile, h, core_out.at[0], core_in.at[root, chunk], sibling)

    def columns(half, chunk):
        return pl.ds(pl.multiple_of(chunk * 2 * WIDTH + half * WIDTH, WIDTH), WIDTH)

    def rhs_copy(half, chunk, slot):
        return pltpu.make_async_copy(rhs.at[:, columns(half, chunk)], rhs_v.at[slot, chunk], local.at[slot, chunk])

    def rhs_swap(chunk):
        return pltpu.make_async_remote_copy(
            src_ref=rhs.at[:, columns(1 - core, chunk)],
            dst_ref=rhs_v.at[core, chunk],
            send_sem=swap_out.at[chunk],
            recv_sem=swap_in.at[chunk],
            device_id=sibling,
            device_id_type=MESH,
        )

    panel_copy = pltpu.make_async_copy(panel, panel_v.at[core], local.at[0, CHUNKS])
    panel_swap = pltpu.make_async_remote_copy(
        src_ref=panel,
        dst_ref=panel_v.at[core],
        send_sem=swap_out.at[CHUNKS],
        recv_sem=swap_in.at[CHUNKS],
        device_id=sibling,
        device_id_type=MESH,
    )
    dinv_copy = pltpu.make_async_copy(dinv.at[pl.ds(2 * lax.rem(me // 2, 2), 2)], dinv_v, local.at[1, CHUNKS])

    peers = [(moved(at, axis, by), core) for axis in "xyz" for by in (1, 2, 3)]
    peers.append((at, 1 - core))
    barrier = pltpu.get_barrier_semaphore()
    for where, which in peers:
        pl.semaphore_signal(barrier, inc=1, device_id=device(where, which), device_id_type=MESH)
    at_second = {"x": jnp.int32(1), "y": jnp.int32(0), "z": jnp.int32(0)}
    relay = (at["x"] == 0) & ((at["y"] == 0) != (at["z"] == 0))

    @pl.when(second_root)
    def _():
        for axis in "yz":
            for j in (1, 2, 3):
                where = {"x": jnp.int32(0), "y": jnp.int32(0), "z": jnp.int32(0)}
                where[axis] = jnp.int32(j)
                pl.semaphore_signal(barrier, inc=1, device_id=device(where, core), device_id_type=MESH)

    def split_dinv():
        dinv_copy.wait()
        for i in range(2):
            one, two, three = split(dinv_v[i])
            for n, part in enumerate((one, one, one, two, two, three)):
                parts[i, :, n * NB : (n + 1) * NB] = part

    def product(i, work):
        one, two, three = split(work)
        right = jnp.concatenate([one, two, three, one, two, one], axis=0)
        return dot(parts[i], right).astype(jnp.bfloat16)

    def keep(block, tile, solved):
        for n in range(SIDE):
            buf[block, tile + n] = solved[:, n * TW : (n + 1) * TW]

    @pl.when(first_root)
    def _():
        dinv_copy.start()
        for chunk in range(CHUNKS):
            for half in range(2):
                rhs_copy(half, chunk, half).start()
        panel_copy.start()
        split_dinv()

    @pl.when(me == 0)
    def _():
        def one(chunk, _):
            for half in range(2):
                rhs_copy(half, chunk, half).wait()
                keep(0, chunk * PER + half * SIDE, product(0, rhs_v[half, chunk]))
            return 0

        lax.fori_loop(0, CHUNKS, one, 0)
        panel_copy.wait()

    @pl.when(second_root)
    def _():
        dinv_copy.start()
        for chunk in range(CHUNKS):
            rhs_copy(core, chunk, core).start()
        panel_copy.start()
        split_dinv()

    pl.semaphore_wait(barrier, len(peers) + jnp.where(relay, 1, 0))

    @pl.when(second_root)
    def _():
        panel_swap.start()
        for chunk in range(CHUNKS):
            rhs_swap(chunk).start()

    def inject(root, chunk, index, h):
        axis, j = KINDS[index]
        if axis == "x":
            j = 2 - root + j
        block, tile = spot(root, chunk, index)
        to = device(moved(at, axis, j), core)
        send(block, tile, h, sent.at[root, 3], got.at[root, chunk * PER + index, h], to)

    @pl.when(me == 0)
    def _():
        def one(chunk, _):
            for h in range(PIECES):
                for index in range(PER):
                    pass_over(0, chunk, index, h)
                    inject(0, chunk, index, h)
            return 0

        lax.fori_loop(0, CHUNKS, one, 0)

    @pl.when(me == 1)
    def _():
        def one(chunk, _):
            wait_tiles(PER, core_in.at[0, chunk])

            @pl.when(chunk == 0)
            def _():
                panel_copy.wait()

            for half in range(2):
                rhs_copy(half, chunk, half).wait()
                first = chunk * PER + half * SIDE
                low = jnp.concatenate([buf[0, first + n] for n in range(SIDE)], axis=1)
                keep(1, first, product(1, rhs_v[half, chunk] - dot(panel_v[1, :, :NB], low)))
                for h in range(PIECES):
                    for n in range(SIDE):
                        inject(0, chunk, half * SIDE + n, h)
                        pass_over(0, chunk, half * SIDE + n, h)
            return 0

        lax.fori_loop(0, CHUNKS, one, 0)

    @pl.when(second_root)
    def _():
        def one(chunk, _):
            for h in range(PIECES):
                for index in range(PER):
                    take(0, chunk, index, h)
                    pass_over(0, chunk, index, h)
            rhs_copy(core, chunk, core).wait()
            wait(rhs_v.at[0, 0], swap_in.at[chunk])

            @pl.when(chunk == 0)
            def _():
                panel_copy.wait()
                wait(panel_v.at[0], swap_in.at[CHUNKS])

            wait_tiles(PER, core_in.at[0, chunk])
            first = chunk * PER + core * SIDE
            low = [jnp.concatenate([buf[b, first + n] for n in range(SIDE)], axis=1) for b in range(2)]
            for i in range(2):
                work = rhs_v[i, chunk]
                for before, block in enumerate(low):
                    work = work - dot(panel_v[i, :, before * NB : (before + 1) * NB], block)
                solved = product(i, work)
                low.append(solved)
                keep(2 + i, first, solved)
                for h in range(PIECES):
                    for n in range(SIDE):
                        inject(1, chunk, i * SIDE + n, h)
                for h in range(PIECES):
                    for n in range(SIDE):
                        pass_over(1, chunk, i * SIDE + n, h)
            return 0

        lax.fori_loop(0, CHUNKS, one, 0)

    def role(root, axis):
        rel = {"x": (at["x"] - root + 4) % 4, "y": at["y"], "z": at["z"]}
        one, two = (rel[name] for name in PLANE[axis])
        a = rel[axis]
        if axis == "x":
            index = jnp.where(a == 2 - root, 2, 5)
            inside = (a == 2 - root) | (a == 3 - root)
        else:
            index = jnp.where(a == 1, 0, jnp.where(a == 2, 6, 3)) + (1 if axis == "z" else 0)
            inside = a != 0
        line = (one == 0) & (two == 0)
        even = jnp.where(line, 0, jnp.where(two == 0, 1, 2))
        odd = jnp.where(line, 0, jnp.where(one == 0, 1, 2))
        none = jnp.int32(-1)
        even, odd = jnp.where(inside, even, none), jnp.where(inside, odd, none)
        near = (at["x"] == 1) & (rel["z" if axis == "y" else "y"] == 0) if root == 0 and axis != "x" else False
        return a, index, inside, line, (one != 0) & (two != 0), even, odd, near

    table = {axis: [role(root, axis) for root in range(ROOTS)] for axis in "xyz"}
    here = [(at["x"] == root) & (at["y"] == 0) & (at["z"] == 0) for root in range(ROOTS)]

    def forward(axis, root, chunk, h, stage):
        first = root == 0
        parity = chunk % 2 == 0
        pick = [jnp.where(first, p, q) for p, q in zip(table[axis][0][:2], table[axis][1][:2])]
        a, index = pick
        even, odd = (jnp.where(first, table[axis][0][n], table[axis][1][n]) for n in (5, 6))
        mine = jnp.where(parity, even, odd)
        near = first & table[axis][0][7]
        one, two = PLANE[axis]
        index_axis = "xyz".index(axis)

        @pl.when(mine == stage)
        def _():
            block, tile = spot(root, chunk, index)
            sem = sent.at[root, index_axis]
            arrived = got.at[root, chunk * PER + index, h]
            take(root, chunk, index, h)

            def along(p, q, by):
                p, q = device(moved(at, p, by), core), device(moved(at, q, by), core)
                return tuple(jnp.where(parity, i, j) for i, j in zip(p, q))

            if axis != "x":

                @pl.when((stage == 0) & first)
                def _():
                    send(block, tile, h, sem, arrived, device(at_second, core))

            @pl.when(stage == 0)
            def _():
                for by in (1, 3, 2):
                    send(block, tile, h, sem, arrived, along(one, two, by))

            @pl.when(stage <= 1)
            def _():
                for by in (1, 3, 2):
                    send(block, tile, h, sem, arrived, along(two, one, by))

            for by in (1, 3, 2):

                @pl.when(((stage != 0) & jnp.logical_not(near)) | ((a + by) % 4 != 0))
                def _():
                    send(block, tile, h, sem, arrived, device(moved(at, axis, by), core))

            pass_over(root, chunk, index, h)

    def receive(index, root, chunk, h):
        axis, j = KINDS[index]
        a = jnp.where(root == 0, table[axis][0][0], table[axis][1][0])
        if axis == "x":
            j = 2 - root + j
        at_root = jnp.where(root == 0, here[0], here[1])

        @pl.when((a != j) & jnp.logical_not(at_root))
        def _():
            take(root, chunk, index, h)
            pass_over(root, chunk, index, h)

    def unit(g):
        return g // UNITS, g % UNITS // PIECES, g % PIECES

    def step(t, _):
        def sub(stage, _):
            g = t - STRIDE * stage

            @pl.when((g >= 0) & (g < ROOTS * UNITS) & jnp.logical_not(second_root & (g < UNITS)))
            def _():
                root, chunk, h = unit(g)
                for axis in "xyz":
                    forward(axis, root, chunk, h, stage)

            return 0

        lax.fori_loop(0, 3, sub, 0)
        g = t - LATE

        @pl.when((g >= 0) & (g < ROOTS * UNITS) & jnp.logical_not(second_root & (g < UNITS)))
        def _():
            root, chunk, h = unit(g)
            for index in range(PER):
                receive(index, root, chunk, h)

        return 0

    lax.fori_loop(0, ROOTS * UNITS + LATE, step, 0)

    for chunk in range(CHUNKS):

        @pl.when((me == 0) | (me > 3))
        def _():
            wait_tiles(PER, core_in.at[0, chunk])

        wait_tiles(PER, core_in.at[1, chunk])

    wait_tiles(2 * TILES, core_out.at[0])
    for root in range(ROOTS):

        @pl.when(here[root])
        def _():
            wait_tiles(TILES, sent.at[root, 3])

        for n, axis in enumerate("xyz"):
            _, _, inside, line, inner, _, _, near = table[axis][root]
            sem = sent.at[root, n]
            straight = root == 0 and axis != "x"

            @pl.when(inside & line)
            def _():
                wait_tiles(CHUNKS * (9 if straight else 8), sem)

            @pl.when(inside & inner)
            def _():
                wait_tiles(CHUNKS * 3, sem)

            edge = inside & jnp.logical_not(line | inner)

            @pl.when(edge & jnp.logical_not(near))
            def _():
                wait_tiles(CHUNKS // 2 * 9, sem)

            if straight:

                @pl.when(edge & near)
                def _():
                    wait_tiles(CHUNKS // 2 * 7, sem)

    @pl.when(second_root)
    def _():
        panel_swap.wait_send()
        for chunk in range(CHUNKS):
            rhs_swap(chunk).wait_send()


def spread(rhs, panel, dinv):
    any_space = pl.BlockSpec(memory_space=pl.ANY)
    rhs, panel, dinv = (pltpu.with_memory_space_constraint(array, pltpu.HBM) for array in (rhs, panel, dinv))
    sem = pltpu.SemaphoreType.DMA
    return pl.pallas_call(
        spread_kernel,
        out_shape=pltpu.VMEM((4, TILES, NB, TW), jnp.bfloat16),
        in_specs=[any_space] * 3,
        out_specs=pl.BlockSpec(memory_space=pltpu.VMEM),
        scratch_shapes=[
            pltpu.VMEM((2, CHUNKS, NB, WIDTH), jnp.float32),
            pltpu.VMEM((2, NB, 4 * NB), jnp.bfloat16),
            pltpu.VMEM((2, NB, NB), jnp.float32),
            pltpu.VMEM((2, NB, 6 * NB), jnp.bfloat16),
            sem((2, CHUNKS + 1)),
            sem((CHUNKS + 1,)),
            sem((CHUNKS + 1,)),
            sem((ROOTS, TILES, PIECES)),
            sem((ROOTS, CHUNKS)),
            sem((1,)),
            sem((ROOTS, 4)),
        ],
        name="spread",
        compiler_params=pltpu.CompilerParams(
            collective_id=1, has_side_effects=True, vmem_limit_bytes=16 * 2**20
        ),
    )(rhs, panel, dinv)


GROUP = 4
WIDE = GROUP * TW
GROUPS = TILES // GROUP


def finish_kernel(buf, rhs, panel, sol, trail, stage, tstage, rhs_v, panel_v, load, out_s, out_t):
    me = lax.axis_index("row") * 8 + lax.axis_index("col")

    def rhs_copy(g):
        cols = pl.ds(g * WIDE, WIDE)
        return pltpu.make_async_copy(rhs.at[:, cols], rhs_v.at[:, cols], load.at[g])

    panel_copy = pltpu.make_async_copy(panel, panel_v, load.at[GROUPS])
    panel_copy.start()
    for g in range(GROUPS):
        rhs_copy(g).start()

    def sol_copy(g):
        return pltpu.make_async_copy(stage.at[g % 2], sol.at[:, pl.ds(g * WIDE, WIDE)], out_s.at[g % 2])

    def trail_copy(g):
        return pltpu.make_async_copy(tstage.at[g % 2], trail.at[:, pl.ds(g * WIDE, WIDE)], out_t.at[g % 2])

    for g in range(GROUPS):
        if g >= 2:
            sol_copy(g - 2).wait()
        for block in range(4):
            for i in range(GROUP):
                stage[g % 2, block * NB : (block + 1) * NB, i * TW : (i + 1) * TW] = buf[
                    block, g * GROUP + i
                ].astype(jnp.float32)
        sol_copy(g).start()
        if g == 0:
            panel_copy.wait()
            for block in range(4):
                cols = slice(block * NB, (block + 1) * NB)
                panel_v[:, cols] = jnp.where(me > block, panel_v[:, cols], jnp.zeros((NB, NB), jnp.bfloat16))
        rhs_copy(g).wait()
        if g >= 2:
            trail_copy(g - 2).wait()
        work = rhs_v[:, g * WIDE : (g + 1) * WIDE]
        for block in range(4):
            low = jnp.concatenate([buf[block, g * GROUP + i] for i in range(GROUP)], axis=1)
            work = work - jnp.dot(
                panel_v[:, block * NB : (block + 1) * NB], low, preferred_element_type=jnp.float32
            )
        tstage[g % 2] = work
        trail_copy(g).start()
    for g in (GROUPS - 2, GROUPS - 1):
        sol_copy(g).wait()
        trail_copy(g).wait()


def finish(buf, rhs, panel):
    any_space = pl.BlockSpec(memory_space=pl.ANY)
    buf = pltpu.with_memory_space_constraint(buf, pltpu.VMEM)
    return pl.pallas_call(
        finish_kernel,
        out_shape=(
            jax.ShapeDtypeStruct((4 * NB, TILES * TW), jnp.float32),
            jax.ShapeDtypeStruct((NB, TILES * TW), jnp.float32),
        ),
        in_specs=[pl.BlockSpec(memory_space=pltpu.VMEM), any_space, any_space],
        out_specs=(any_space, any_space),
        scratch_shapes=[
            pltpu.VMEM((2, 4 * NB, WIDE), jnp.float32),
            pltpu.VMEM((2, NB, WIDE), jnp.float32),
            pltpu.VMEM((NB, TILES * TW), jnp.float32),
            pltpu.VMEM((NB, 4 * NB), jnp.bfloat16),
            pltpu.SemaphoreType.DMA((GROUPS + 1,)),
            pltpu.SemaphoreType.DMA((2,)),
            pltpu.SemaphoreType.DMA((2,)),
        ],
        name="finish",
        compiler_params=pltpu.CompilerParams(vmem_limit_bytes=24 * 2**20),
    )(buf, rhs, panel)


def body(rhs, panel, diag_inverse):
    own = rhs.reshape(rhs.shape[2], rhs.shape[3])
    factor = panel.reshape(panel.shape[2], panel.shape[3])
    tiles = spread(own, factor, diag_inverse)
    solved, trailing = finish(tiles, own, factor)
    return solved, trailing.reshape(rhs.shape)


def solution(mesh):
    in_specs = (P(None, ("row", "col"), None, None), P(None, ("row", "col"), None, None), P())
    out_specs = (P(), P(None, ("row", "col"), None, None))
    return jax.shard_map(body, mesh=mesh, in_specs=in_specs, out_specs=out_specs, check_vma=False)
```

```python
import jax
import jax.numpy as jnp
from jax import lax
from jax.experimental import pallas as pl
from jax.experimental.pallas import tpu as pltpu
from jax.sharding import PartitionSpec as P

MESH = pl.DeviceIdType.MESH
NB = 256
TW = 128
TILES = 32
PER = 8
SIDE = PER // 2
CHUNKS = TILES // PER
ROOTS = 2
WIDTH = SIDE * TW
PIECES = 2
ROWS = NB // PIECES
UNITS = CHUNKS * PIECES
STRIDE = 4
LATE = 14
WINDOW = 1
KINDS = (("y", 1), ("z", 1), ("x", 0), ("y", 3), ("z", 3), ("x", 1), ("y", 2), ("z", 2))
PLANE = {"x": ("z", "y"), "y": ("x", "z"), "z": ("y", "x")}


def place():
    row, col = lax.axis_index("row"), lax.axis_index("col")
    return {"z": row // 4, "y": row % 4, "x": col // 2}, col % 2


def device(at, core):
    return (at["z"] * 4 + at["y"], at["x"] * 2 + core)


def moved(at, axis, by):
    new = dict(at)
    new[axis] = (at[axis] + by) % 4
    return new


def split(value):
    first = value.astype(jnp.bfloat16)
    rest = value - first.astype(jnp.float32)
    second = rest.astype(jnp.bfloat16)
    third = (rest - second.astype(jnp.float32)).astype(jnp.bfloat16)
    return first, second, third


def dot(left, right):
    return jnp.dot(left, right, preferred_element_type=jnp.float32)


def spread_kernel(
    rhs, panel, dinv, buf, rhs_v, panel_v, dinv_v, parts, mixed, local, swap_out, swap_in, got, core_in, core_out, sent, sent_root
):
    at, core = place()
    me = lax.axis_index("row") * 8 + lax.axis_index("col")
    sibling = device(at, 1 - core)
    first_root, second_root = me // 2 == 0, me // 2 == 1

    def spot(root, chunk, index):
        block = jnp.where(root == 0, core, 2 + index // SIDE)
        tile = chunk * PER + jnp.where(root == 0, index, core * SIDE + index % SIDE)
        return block, tile

    def send(block, tile, h, send_sem, recv_sem, to):
        piece = buf.at[block, tile, pl.ds(pl.multiple_of(h * ROWS, ROWS), ROWS)]
        pltpu.make_async_remote_copy(
            src_ref=piece,
            dst_ref=piece,
            send_sem=send_sem,
            recv_sem=recv_sem,
            device_id=to,
            device_id_type=MESH,
        ).start()

    def wait(ref, sem):
        pltpu.make_async_copy(ref, ref, sem).wait()

    def wait_tiles(count, sem):
        wait(buf.at[pl.ds(0, 2), pl.ds(0, count // 2)], sem)

    def take(root, chunk, index, h):
        wait(buf.at[0, 0, pl.ds(0, ROWS)], got.at[root, chunk * PER + index, h])

    def pass_over(root, chunk, index, h):
        block, tile = spot(root, chunk, index)
        send(block, tile, h, core_out.at[0], core_in.at[root, chunk], sibling)

    def pass_row(root, chunk, block, first, count):
        row = buf.at[block, pl.ds(first, count)]
        pltpu.make_async_remote_copy(
            src_ref=row,
            dst_ref=row,
            send_sem=core_out.at[0],
            recv_sem=core_in.at[root, chunk],
            device_id=sibling,
            device_id_type=MESH,
        ).start()

    def columns(half, chunk):
        return pl.ds(pl.multiple_of(chunk * 2 * WIDTH + half * WIDTH, WIDTH), WIDTH)

    def rhs_copy(half, chunk, slot):
        return pltpu.make_async_copy(rhs.at[:, columns(half, chunk)], rhs_v.at[slot, chunk], local.at[slot, chunk])

    def rhs_swap(chunk):
        return pltpu.make_async_remote_copy(
            src_ref=rhs.at[:, columns(1 - core, chunk)],
            dst_ref=rhs_v.at[core, chunk],
            send_sem=swap_out.at[chunk],
            recv_sem=swap_in.at[chunk],
            device_id=sibling,
            device_id_type=MESH,
        )

    panel_copy = pltpu.make_async_copy(panel, panel_v.at[core], local.at[0, CHUNKS])
    panel_swap = pltpu.make_async_remote_copy(
        src_ref=panel,
        dst_ref=panel_v.at[core],
        send_sem=swap_out.at[CHUNKS],
        recv_sem=swap_in.at[CHUNKS],
        device_id=sibling,
        device_id_type=MESH,
    )
    dinv_copy = pltpu.make_async_copy(dinv.at[pl.ds(2 * lax.rem(me // 2, 2), 2)], dinv_v, local.at[1, CHUNKS])

    peers = [(moved(at, axis, by), core) for axis in "xyz" for by in (1, 2, 3)]
    peers.append((at, 1 - core))
    barrier = pltpu.get_barrier_semaphore()
    for where, which in peers:
        pl.semaphore_signal(barrier, inc=1, device_id=device(where, which), device_id_type=MESH)
    at_second = {"x": jnp.int32(1), "y": jnp.int32(0), "z": jnp.int32(0)}
    relay = (at["x"] == 0) & ((at["y"] == 0) != (at["z"] == 0))

    @pl.when(second_root)
    def _():
        for axis in "yz":
            for j in (1, 2, 3):
                where = {"x": jnp.int32(0), "y": jnp.int32(0), "z": jnp.int32(0)}
                where[axis] = jnp.int32(j)
                pl.semaphore_signal(barrier, inc=1, device_id=device(where, core), device_id_type=MESH)

    def split_dinv():
        dinv_copy.wait()
        for i in range(2):
            one, two, three = split(dinv_v[i])
            for n, part in enumerate((one, one, one, two, two, three)):
                parts[i, :, n * NB : (n + 1) * NB] = part

    def product(i, work):
        one, two, three = split(work)
        right = jnp.concatenate([one, two, three, one, two, one], axis=0)
        return dot(parts[i], right)

    def mix(i, width):
        factor = panel_v[i, :, :width]
        exact = sum(dot(parts[i, :, n * NB : (n + 1) * NB], factor) for n in (0, 3, 5))
        one, two, _ = split(exact)
        mixed[i, :, :width] = one
        mixed[i, :, width : 2 * width] = two

    def solve(i, start, low):
        width = NB * len(low)
        return (start - dot(mixed[i, :, : 2 * width], jnp.concatenate(low + low, axis=0))).astype(jnp.bfloat16)

    def keep(block, tile, solved):
        for n in range(SIDE):
            buf[block, tile + n] = solved[:, n * TW : (n + 1) * TW]

    @pl.when(first_root)
    def _():
        dinv_copy.start()
        for chunk in range(CHUNKS):
            for half in range(2):
                rhs_copy(half, chunk, half).start()
        panel_copy.start()
        split_dinv()

    @pl.when(me == 0)
    def _():
        def one(chunk, _):
            for half in range(2):
                rhs_copy(half, chunk, half).wait()
                keep(0, chunk * PER + half * SIDE, product(0, rhs_v[half, chunk]).astype(jnp.bfloat16))
            return 0

        lax.fori_loop(0, CHUNKS, one, 0)
        panel_copy.wait()

    @pl.when(me == 1)
    def _():
        panel_copy.wait()
        mix(1, NB)

        def one(chunk, _):
            for half in range(2):
                rhs_copy(half, chunk, half).wait()
                rhs_v[half, chunk] = product(1, rhs_v[half, chunk])
            return 0

        lax.fori_loop(0, CHUNKS, one, 0)

    @pl.when(second_root)
    def _():
        dinv_copy.start()
        for chunk in range(CHUNKS):
            rhs_copy(core, chunk, core).start()
        panel_copy.start()
        split_dinv()

    pl.semaphore_wait(barrier, len(peers) + jnp.where(relay, 1, 0))

    @pl.when(second_root)
    def _():
        panel_swap.start()
        for chunk in range(CHUNKS):
            rhs_swap(chunk).start()

    def inject(root, chunk, index, h):
        axis, j = KINDS[index]
        if axis == "x":
            j = 2 - root + j
        block, tile = spot(root, chunk, index)
        to = device(moved(at, axis, j), core)
        send(block, tile, h, sent_root.at[chunk], got.at[root, chunk * PER + index, h], to)

    @pl.when(me == 0)
    def _():
        def one(chunk, _):
            @pl.when(chunk >= WINDOW)
            def _():
                wait_tiles(PER, sent_root.at[chunk - WINDOW])

            pass_row(0, chunk, 0, chunk * PER, PER)
            for h in range(PIECES):
                for index in range(PER):
                    inject(0, chunk, index, h)
            return 0

        lax.fori_loop(0, CHUNKS, one, 0)

    @pl.when(me == 1)
    def _():
        def one(chunk, _):
            wait_tiles(PER, core_in.at[0, chunk])
            for half in range(2):
                first = chunk * PER + half * SIDE
                low = jnp.concatenate([buf[0, first + n] for n in range(SIDE)], axis=1)
                keep(1, first, solve(1, rhs_v[half, chunk], [low]))
                for h in range(PIECES):
                    for n in range(SIDE):
                        inject(0, chunk, half * SIDE + n, h)
                pass_row(0, chunk, 1, first, SIDE)
            return 0

        lax.fori_loop(0, CHUNKS, one, 0)

    @pl.when(second_root)
    def _():
        panel_copy.wait()
        wait(panel_v.at[0], swap_in.at[CHUNKS])
        mix(0, 2 * NB)
        mix(1, 3 * NB)

        def start(chunk, _):
            rhs_copy(core, chunk, core).wait()
            wait(rhs_v.at[0, 0], swap_in.at[chunk])
            for i in range(2):
                rhs_v[i, chunk] = product(i, rhs_v[i, chunk])
            return 0

        lax.fori_loop(0, CHUNKS, start, 0)

        def one(chunk, _):
            for h in range(PIECES):
                for index in range(PER):
                    take(0, chunk, index, h)
                    pass_over(0, chunk, index, h)
            wait_tiles(PER, core_in.at[0, chunk])
            first = chunk * PER + core * SIDE
            low = [jnp.concatenate([buf[b, first + n] for n in range(SIDE)], axis=1) for b in range(2)]
            for i in range(2):
                solved = solve(i, rhs_v[i, chunk], low)
                low.append(solved)
                keep(2 + i, first, solved)
                for h in range(PIECES):
                    for n in range(SIDE):
                        inject(1, chunk, i * SIDE + n, h)
                pass_row(1, chunk, 2 + i, first, SIDE)
            return 0

        lax.fori_loop(0, CHUNKS, one, 0)

    def role(root, axis):
        rel = {"x": (at["x"] - root + 4) % 4, "y": at["y"], "z": at["z"]}
        one, two = (rel[name] for name in PLANE[axis])
        a = rel[axis]
        if axis == "x":
            index = jnp.where(a == 2 - root, 2, 5)
            inside = (a == 2 - root) | (a == 3 - root)
        else:
            index = jnp.where(a == 1, 0, jnp.where(a == 2, 6, 3)) + (1 if axis == "z" else 0)
            inside = a != 0
        line = (one == 0) & (two == 0)
        even = jnp.where(line, 0, jnp.where(two == 0, 1, 2))
        odd = jnp.where(line, 0, jnp.where(one == 0, 1, 2))
        none = jnp.int32(-1)
        even, odd = jnp.where(inside, even, none), jnp.where(inside, odd, none)
        near = (at["x"] == 1) & (rel["z" if axis == "y" else "y"] == 0) if root == 0 and axis != "x" else False
        return a, index, inside, line, (one != 0) & (two != 0), even, odd, near

    table = {axis: [role(root, axis) for root in range(ROOTS)] for axis in "xyz"}
    here = [(at["x"] == root) & (at["y"] == 0) & (at["z"] == 0) for root in range(ROOTS)]

    def forward(axis, root, chunk, h, stage):
        first = root == 0
        parity = chunk % 2 == 0
        pick = [jnp.where(first, p, q) for p, q in zip(table[axis][0][:2], table[axis][1][:2])]
        a, index = pick
        even, odd = (jnp.where(first, table[axis][0][n], table[axis][1][n]) for n in (5, 6))
        mine = jnp.where(parity, even, odd)
        near = first & table[axis][0][7]
        one, two = PLANE[axis]
        index_axis = "xyz".index(axis)

        @pl.when(mine == stage)
        def _():
            block, tile = spot(root, chunk, index)
            sem = sent.at[root, index_axis]
            arrived = got.at[root, chunk * PER + index, h]
            take(root, chunk, index, h)

            def along(p, q, by):
                p, q = device(moved(at, p, by), core), device(moved(at, q, by), core)
                return tuple(jnp.where(parity, i, j) for i, j in zip(p, q))

            if axis != "x":

                @pl.when((stage == 0) & first)
                def _():
                    send(block, tile, h, sem, arrived, device(at_second, core))

            @pl.when(stage == 0)
            def _():
                for by in (1, 3, 2):
                    send(block, tile, h, sem, arrived, along(one, two, by))

            @pl.when(stage <= 1)
            def _():
                for by in (1, 3, 2):
                    send(block, tile, h, sem, arrived, along(two, one, by))

            for by in (1, 3, 2):

                @pl.when(((stage != 0) & jnp.logical_not(near)) | ((a + by) % 4 != 0))
                def _():
                    send(block, tile, h, sem, arrived, device(moved(at, axis, by), core))

            pass_over(root, chunk, index, h)

    def receive(index, root, chunk, h):
        axis, j = KINDS[index]
        a = jnp.where(root == 0, table[axis][0][0], table[axis][1][0])
        if axis == "x":
            j = 2 - root + j
        at_root = jnp.where(root == 0, here[0], here[1])

        @pl.when((a != j) & jnp.logical_not(at_root))
        def _():
            take(root, chunk, index, h)
            pass_over(root, chunk, index, h)

    def unit(g):
        return g // UNITS, g % UNITS // PIECES, g % PIECES

    def step(t, _):
        def sub(stage, _):
            g = t - STRIDE * stage

            @pl.when((g >= 0) & (g < ROOTS * UNITS) & jnp.logical_not(second_root & (g < UNITS)))
            def _():
                root, chunk, h = unit(g)
                for axis in "xyz":
                    forward(axis, root, chunk, h, stage)

            return 0

        lax.fori_loop(0, 3, sub, 0)
        g = t - LATE

        @pl.when((g >= 0) & (g < ROOTS * UNITS) & jnp.logical_not(second_root & (g < UNITS)))
        def _():
            root, chunk, h = unit(g)
            for index in range(PER):
                receive(index, root, chunk, h)

        return 0

    lax.fori_loop(0, ROOTS * UNITS + LATE, step, 0)

    for chunk in range(CHUNKS):

        @pl.when((me == 0) | (me > 3))
        def _():
            wait_tiles(PER, core_in.at[0, chunk])

        wait_tiles(PER, core_in.at[1, chunk])

    wait_tiles(2 * TILES, core_out.at[0])

    @pl.when(me < 4)
    def _():
        for chunk in range(CHUNKS):

            @pl.when((me != 0) | (chunk >= CHUNKS - WINDOW))
            def _():
                wait_tiles(PER, sent_root.at[chunk])

    for root in range(ROOTS):

        for n, axis in enumerate("xyz"):
            _, _, inside, line, inner, _, _, near = table[axis][root]
            sem = sent.at[root, n]
            straight = root == 0 and axis != "x"

            @pl.when(inside & line)
            def _():
                wait_tiles(CHUNKS * (9 if straight else 8), sem)

            @pl.when(inside & inner)
            def _():
                wait_tiles(CHUNKS * 3, sem)

            edge = inside & jnp.logical_not(line | inner)

            @pl.when(edge & jnp.logical_not(near))
            def _():
                wait_tiles(CHUNKS // 2 * 9, sem)

            if straight:

                @pl.when(edge & near)
                def _():
                    wait_tiles(CHUNKS // 2 * 7, sem)

    @pl.when(second_root)
    def _():
        panel_swap.wait_send()
        for chunk in range(CHUNKS):
            rhs_swap(chunk).wait_send()


def spread(rhs, panel, dinv):
    any_space = pl.BlockSpec(memory_space=pl.ANY)
    rhs, panel, dinv = (pltpu.with_memory_space_constraint(array, pltpu.HBM) for array in (rhs, panel, dinv))
    sem = pltpu.SemaphoreType.DMA
    return pl.pallas_call(
        spread_kernel,
        out_shape=pltpu.VMEM((4, TILES, NB, TW), jnp.bfloat16),
        in_specs=[any_space] * 3,
        out_specs=pl.BlockSpec(memory_space=pltpu.VMEM),
        scratch_shapes=[
            pltpu.VMEM((2, CHUNKS, NB, WIDTH), jnp.float32),
            pltpu.VMEM((2, NB, 4 * NB), jnp.bfloat16),
            pltpu.VMEM((2, NB, NB), jnp.float32),
            pltpu.VMEM((2, NB, 6 * NB), jnp.bfloat16),
            pltpu.VMEM((2, NB, 6 * NB), jnp.bfloat16),
            sem((2, CHUNKS + 1)),
            sem((CHUNKS + 1,)),
            sem((CHUNKS + 1,)),
            sem((ROOTS, TILES, PIECES)),
            sem((ROOTS, CHUNKS)),
            sem((1,)),
            sem((ROOTS, 3)),
            sem((CHUNKS,)),
        ],
        name="spread",
        compiler_params=pltpu.CompilerParams(
            collective_id=1, has_side_effects=True, vmem_limit_bytes=16 * 2**20
        ),
    )(rhs, panel, dinv)


BAND = 64
BANDS = 4 * NB // BAND
SLOTS = 4
WIDE = PER * TW
GROUPS = CHUNKS


def finish_kernel(buf, rhs, panel, sol, trail, stage, tstage, rhs_v, panel_v, load, out_s, out_t):
    me = lax.axis_index("row") * 8 + lax.axis_index("col")

    def rhs_copy(g):
        cols = pl.ds(g * WIDE, WIDE)
        return pltpu.make_async_copy(rhs.at[:, cols], rhs_v.at[:, cols], load.at[g])

    panel_copy = pltpu.make_async_copy(panel, panel_v, load.at[GROUPS])

    def sol_copy(band):
        rows = pl.ds(band * BAND, BAND)
        return pltpu.make_async_copy(stage.at[band % SLOTS], sol.at[rows], out_s.at[band % SLOTS])

    def trail_copy(g):
        return pltpu.make_async_copy(tstage.at[g % 2], trail.at[:, pl.ds(g * WIDE, WIDE)], out_t.at[g % 2])

    def widen(band):
        if band >= SLOTS:
            sol_copy(band - SLOTS).wait()
        block, first = band * BAND // NB, band * BAND % NB
        for tile in range(TILES):
            stage[band % SLOTS, :, tile * TW : (tile + 1) * TW] = buf[block, tile, first : first + BAND].astype(
                jnp.float32
            )
        sol_copy(band).start()

    def update(g):
        rhs_copy(g).wait()
        if g >= 2:
            trail_copy(g - 2).wait()
        low = [jnp.concatenate([buf[b, g * PER + i] for i in range(PER)], axis=1) for b in range(4)]
        tstage[g % 2] = rhs_v[:, g * WIDE : (g + 1) * WIDE] - dot(panel_v[...], jnp.concatenate(low, axis=0))
        trail_copy(g).start()

    panel_copy.start()
    for g in range(GROUPS):
        rhs_copy(g).start()
    each = BANDS // GROUPS
    for band in range(SLOTS):
        widen(band)
    panel_copy.wait()
    for block in range(4):
        cols = slice(block * NB, (block + 1) * NB)
        panel_v[:, cols] = jnp.where(me > block, panel_v[:, cols], jnp.zeros((NB, NB), jnp.bfloat16))
    for g in range(GROUPS):
        update(g)
        for band in range(SLOTS + g * each, min(SLOTS + (g + 1) * each, BANDS)):
            widen(band)
    for band in range(BANDS - SLOTS, BANDS):
        sol_copy(band).wait()
    for g in range(GROUPS - 2, GROUPS):
        trail_copy(g).wait()


def finish(buf, rhs, panel):
    any_space = pl.BlockSpec(memory_space=pl.ANY)
    buf = pltpu.with_memory_space_constraint(buf, pltpu.VMEM)
    return pl.pallas_call(
        finish_kernel,
        out_shape=(
            jax.ShapeDtypeStruct((4 * NB, TILES * TW), jnp.float32),
            jax.ShapeDtypeStruct((NB, TILES * TW), jnp.float32),
        ),
        in_specs=[pl.BlockSpec(memory_space=pltpu.VMEM), any_space, any_space],
        out_specs=(any_space, any_space),
        scratch_shapes=[
            pltpu.VMEM((SLOTS, BAND, TILES * TW), jnp.float32),
            pltpu.VMEM((2, NB, WIDE), jnp.float32),
            pltpu.VMEM((NB, TILES * TW), jnp.float32),
            pltpu.VMEM((NB, 4 * NB), jnp.bfloat16),
            pltpu.SemaphoreType.DMA((GROUPS + 1,)),
            pltpu.SemaphoreType.DMA((SLOTS,)),
            pltpu.SemaphoreType.DMA((2,)),
        ],
        name="finish",
        compiler_params=pltpu.CompilerParams(vmem_limit_bytes=24 * 2**20),
    )(buf, rhs, panel)


def body(rhs, panel, diag_inverse):
    own = rhs.reshape(rhs.shape[2], rhs.shape[3])
    factor = panel.reshape(panel.shape[2], panel.shape[3])
    tiles = spread(own, factor, diag_inverse)
    solved, trailing = finish(tiles, own, factor)
    return solved, trailing.reshape(rhs.shape)


def solution(mesh):
    in_specs = (P(None, ("row", "col"), None, None), P(None, ("row", "col"), None, None), P())
    out_specs = (P(), P(None, ("row", "col"), None, None))
    return jax.shard_map(body, mesh=mesh, in_specs=in_specs, out_specs=out_specs, check_vma=False)
```

```python
import jax
import jax.numpy as jnp
from jax import lax
from jax.experimental import pallas as pl
from jax.experimental.pallas import tpu as pltpu
from jax.sharding import PartitionSpec as P

MESH = pl.DeviceIdType.MESH
NB = 256
TW = 128
TILES = 32
PER = 8
SIDE = PER // 2
CHUNKS = TILES // PER
ROOTS = 2
WIDTH = SIDE * TW
PIECES = 2
ROWS = NB // PIECES
UNITS = CHUNKS * PIECES
STRIDE = 4
LATE = 14
OFFSET = 6
WINDOW = 1
KINDS = (("y", 2), ("z", 2), ("x", 0), ("y", 1), ("z", 1), ("x", 1), ("y", 3), ("z", 3))
PLANE = {"x": ("z", "y"), "y": ("x", "z"), "z": ("y", "x")}


def place():
    row, col = lax.axis_index("row"), lax.axis_index("col")
    return {"z": row // 4, "y": row % 4, "x": col // 2}, col % 2


def device(at, core):
    return (at["z"] * 4 + at["y"], at["x"] * 2 + core)


def moved(at, axis, by):
    new = dict(at)
    new[axis] = (at[axis] + by) % 4
    return new


def split(value):
    first = value.astype(jnp.bfloat16)
    rest = value - first.astype(jnp.float32)
    second = rest.astype(jnp.bfloat16)
    third = (rest - second.astype(jnp.float32)).astype(jnp.bfloat16)
    return first, second, third


def dot(left, right):
    return jnp.dot(left, right, preferred_element_type=jnp.float32)


def spread_kernel(
    rhs, panel, dinv, buf, rhs_v, panel_v, dinv_v, parts, mixed, local, swap_out, swap_in, got, core_in, core_out, sent, sent_root
):
    at, core = place()
    me = lax.axis_index("row") * 8 + lax.axis_index("col")
    sibling = device(at, 1 - core)
    first_root, second_root = me // 2 == 0, me // 2 == 1

    def spot(root, chunk, index):
        block = jnp.where(root == 0, core, 2 + index // SIDE)
        tile = chunk * PER + jnp.where(root == 0, index, core * SIDE + index % SIDE)
        return block, tile

    def send(block, tile, h, send_sem, recv_sem, to):
        piece = buf.at[block, tile, pl.ds(pl.multiple_of(h * ROWS, ROWS), ROWS)]
        pltpu.make_async_remote_copy(
            src_ref=piece,
            dst_ref=piece,
            send_sem=send_sem,
            recv_sem=recv_sem,
            device_id=to,
            device_id_type=MESH,
        ).start()

    def wait(ref, sem):
        pltpu.make_async_copy(ref, ref, sem).wait()

    def wait_tiles(count, sem):
        wait(buf.at[pl.ds(0, 2), pl.ds(0, count // 2)], sem)

    def take(root, chunk, index, h):
        wait(buf.at[0, 0, pl.ds(0, ROWS)], got.at[root, chunk * PER + index, h])

    def pass_over(root, chunk, index, h):
        block, tile = spot(root, chunk, index)
        send(block, tile, h, core_out.at[0], core_in.at[root, chunk], sibling)

    def pass_row(root, chunk, block, first, count):
        row = buf.at[block, pl.ds(first, count)]
        pltpu.make_async_remote_copy(
            src_ref=row,
            dst_ref=row,
            send_sem=core_out.at[0],
            recv_sem=core_in.at[root, chunk],
            device_id=sibling,
            device_id_type=MESH,
        ).start()

    def columns(half, chunk):
        return pl.ds(pl.multiple_of(chunk * 2 * WIDTH + half * WIDTH, WIDTH), WIDTH)

    def rhs_copy(half, chunk, slot):
        return pltpu.make_async_copy(rhs.at[:, columns(half, chunk)], rhs_v.at[slot, chunk], local.at[slot, chunk])

    def rhs_swap(chunk):
        return pltpu.make_async_remote_copy(
            src_ref=rhs.at[:, columns(1 - core, chunk)],
            dst_ref=rhs_v.at[core, chunk],
            send_sem=swap_out.at[chunk],
            recv_sem=swap_in.at[chunk],
            device_id=sibling,
            device_id_type=MESH,
        )

    panel_copy = pltpu.make_async_copy(panel, panel_v.at[core], local.at[0, CHUNKS])
    panel_swap = pltpu.make_async_remote_copy(
        src_ref=panel,
        dst_ref=panel_v.at[core],
        send_sem=swap_out.at[CHUNKS],
        recv_sem=swap_in.at[CHUNKS],
        device_id=sibling,
        device_id_type=MESH,
    )
    dinv_copy = pltpu.make_async_copy(dinv.at[pl.ds(2 * lax.rem(me // 2, 2), 2)], dinv_v, local.at[1, CHUNKS])

    peers = [(moved(at, axis, by), core) for axis in "xyz" for by in (1, 2, 3)]
    peers.append((at, 1 - core))
    barrier = pltpu.get_barrier_semaphore()
    for where, which in peers:
        pl.semaphore_signal(barrier, inc=1, device_id=device(where, which), device_id_type=MESH)
    at_second = {"x": jnp.int32(1), "y": jnp.int32(0), "z": jnp.int32(0)}
    relay = (at["x"] == 0) & ((at["y"] == 0) != (at["z"] == 0))

    @pl.when(second_root)
    def _():
        for axis in "yz":
            for j in (1, 2, 3):
                where = {"x": jnp.int32(0), "y": jnp.int32(0), "z": jnp.int32(0)}
                where[axis] = jnp.int32(j)
                pl.semaphore_signal(barrier, inc=1, device_id=device(where, core), device_id_type=MESH)

    def split_dinv():
        dinv_copy.wait()
        for i in range(2):
            one, two, three = split(dinv_v[i])
            for n, part in enumerate((one, one, one, two, two, three)):
                parts[i, :, n * NB : (n + 1) * NB] = part

    def product(i, work):
        one, two, three = split(work)
        right = jnp.concatenate([one, two, three, one, two, one], axis=0)
        return dot(parts[i], right)

    def mix(i, width):
        factor = panel_v[i, :, :width]
        exact = sum(dot(parts[i, :, n * NB : (n + 1) * NB], factor) for n in (0, 3, 5))
        one, two, _ = split(exact)
        mixed[i, :, :width] = one
        mixed[i, :, width : 2 * width] = two

    def solve(i, start, low):
        width = NB * len(low)
        return (start - dot(mixed[i, :, : 2 * width], jnp.concatenate(low + low, axis=0))).astype(jnp.bfloat16)

    def keep(block, tile, solved):
        for n in range(SIDE):
            buf[block, tile + n] = solved[:, n * TW : (n + 1) * TW]

    @pl.when(first_root)
    def _():
        dinv_copy.start()
        for chunk in range(CHUNKS):
            for half in range(2):
                rhs_copy(half, chunk, half).start()
        panel_copy.start()
        split_dinv()

    @pl.when(me == 0)
    def _():
        def one(chunk, _):
            for half in range(2):
                rhs_copy(half, chunk, half).wait()
                keep(0, chunk * PER + half * SIDE, product(0, rhs_v[half, chunk]).astype(jnp.bfloat16))
            return 0

        lax.fori_loop(0, CHUNKS, one, 0)
        panel_copy.wait()

    @pl.when(me == 1)
    def _():
        panel_copy.wait()
        mix(1, NB)

        def one(chunk, _):
            for half in range(2):
                rhs_copy(half, chunk, half).wait()
                rhs_v[half, chunk] = product(1, rhs_v[half, chunk])
            return 0

        lax.fori_loop(0, CHUNKS, one, 0)

    @pl.when(second_root)
    def _():
        dinv_copy.start()
        for chunk in range(CHUNKS):
            rhs_copy(core, chunk, core).start()
        panel_copy.start()
        split_dinv()

    pl.semaphore_wait(barrier, len(peers) + jnp.where(relay, 1, 0))

    @pl.when(second_root)
    def _():
        panel_swap.start()
        for chunk in range(CHUNKS):
            rhs_swap(chunk).start()

    def inject(root, chunk, index, h):
        axis, j = KINDS[index]
        if axis == "x":
            j = 2 - root + j
        block, tile = spot(root, chunk, index)
        to = device(moved(at, axis, j), core)
        send(block, tile, h, sent_root.at[chunk], got.at[root, chunk * PER + index, h], to)

    @pl.when(me == 0)
    def _():
        def one(chunk, _):
            @pl.when(chunk >= WINDOW)
            def _():
                wait_tiles(PER, sent_root.at[chunk - WINDOW])

            pass_row(0, chunk, 0, chunk * PER, PER)
            for h in range(PIECES):
                for index in range(PER):
                    inject(0, chunk, index, h)
            return 0

        lax.fori_loop(0, CHUNKS, one, 0)

    @pl.when(me == 1)
    def _():
        def one(chunk, _):
            wait_tiles(PER, core_in.at[0, chunk])
            for half in range(2):
                first = chunk * PER + half * SIDE
                low = jnp.concatenate([buf[0, first + n] for n in range(SIDE)], axis=1)
                keep(1, first, solve(1, rhs_v[half, chunk], [low]))
                for h in range(PIECES):
                    for n in range(SIDE):
                        inject(0, chunk, half * SIDE + n, h)
                pass_row(0, chunk, 1, first, SIDE)
            return 0

        lax.fori_loop(0, CHUNKS, one, 0)

    @pl.when(second_root)
    def _():
        panel_copy.wait()
        wait(panel_v.at[0], swap_in.at[CHUNKS])
        mix(0, 2 * NB)
        mix(1, 3 * NB)

        def start(chunk, _):
            rhs_copy(core, chunk, core).wait()
            wait(rhs_v.at[0, 0], swap_in.at[chunk])
            for i in range(2):
                rhs_v[i, chunk] = product(i, rhs_v[i, chunk])
            return 0

        lax.fori_loop(0, CHUNKS, start, 0)

        def one(chunk, _):
            for h in range(PIECES):
                for index in range(PER):
                    take(0, chunk, index, h)
                    pass_over(0, chunk, index, h)
            wait_tiles(PER, core_in.at[0, chunk])
            first = chunk * PER + core * SIDE
            low = [jnp.concatenate([buf[b, first + n] for n in range(SIDE)], axis=1) for b in range(2)]
            for i in range(2):
                solved = solve(i, rhs_v[i, chunk], low)
                low.append(solved)
                keep(2 + i, first, solved)
                for h in range(PIECES):
                    for n in range(SIDE):
                        inject(1, chunk, i * SIDE + n, h)
                pass_row(1, chunk, 2 + i, first, SIDE)
            return 0

        lax.fori_loop(0, CHUNKS, one, 0)

    def role(root, axis):
        rel = {"x": (at["x"] - root + 4) % 4, "y": at["y"], "z": at["z"]}
        one, two = (rel[name] for name in PLANE[axis])
        a = rel[axis]
        if axis == "x":
            index = jnp.where(a == 2 - root, 2, 5)
            inside = (a == 2 - root) | (a == 3 - root)
        else:
            index = jnp.where(a == 2, 0, jnp.where(a == 1, 3, 6)) + (1 if axis == "z" else 0)
            inside = a != 0
        line = (one == 0) & (two == 0)
        even = jnp.where(line, 0, jnp.where(two == 0, 1, 2))
        odd = jnp.where(line, 0, jnp.where(one == 0, 1, 2))
        none = jnp.int32(-1)
        even, odd = jnp.where(inside, even, none), jnp.where(inside, odd, none)
        near = (at["x"] == 1) & (rel["z" if axis == "y" else "y"] == 0) if root == 0 and axis != "x" else False
        return a, index, inside, line, (one != 0) & (two != 0), even, odd, near

    table = {axis: [role(root, axis) for root in range(ROOTS)] for axis in "xyz"}
    here = [(at["x"] == root) & (at["y"] == 0) & (at["z"] == 0) for root in range(ROOTS)]

    def forward(axis, root, chunk, h, stage):
        first = root == 0
        parity = chunk % 2 == 0
        pick = [jnp.where(first, p, q) for p, q in zip(table[axis][0][:2], table[axis][1][:2])]
        a, index = pick
        even, odd = (jnp.where(first, table[axis][0][n], table[axis][1][n]) for n in (5, 6))
        mine = jnp.where(parity, even, odd)
        near = first & table[axis][0][7]
        one, two = PLANE[axis]
        index_axis = "xyz".index(axis)

        @pl.when(mine == stage)
        def _():
            block, tile = spot(root, chunk, index)
            sem = sent.at[root, index_axis]
            arrived = got.at[root, chunk * PER + index, h]
            take(root, chunk, index, h)

            def along(p, q, by):
                p, q = device(moved(at, p, by), core), device(moved(at, q, by), core)
                return tuple(jnp.where(parity, i, j) for i, j in zip(p, q))

            if axis != "x":

                @pl.when((stage == 0) & first)
                def _():
                    send(block, tile, h, sem, arrived, device(at_second, core))

            @pl.when(stage == 0)
            def _():
                for by in (1, 3, 2):
                    send(block, tile, h, sem, arrived, along(one, two, by))

            @pl.when(stage <= 1)
            def _():
                for by in (1, 3, 2):
                    send(block, tile, h, sem, arrived, along(two, one, by))

            for by in (1, 3, 2):

                @pl.when(((stage != 0) & jnp.logical_not(near)) | ((a + by) % 4 != 0))
                def _():
                    send(block, tile, h, sem, arrived, device(moved(at, axis, by), core))

            pass_over(root, chunk, index, h)

    def receive(index, root, chunk, h):
        axis, j = KINDS[index]
        a = jnp.where(root == 0, table[axis][0][0], table[axis][1][0])
        if axis == "x":
            j = 2 - root + j
        at_root = jnp.where(root == 0, here[0], here[1])

        @pl.when((a != j) & jnp.logical_not(at_root))
        def _():
            take(root, chunk, index, h)
            pass_over(root, chunk, index, h)

    def step(t, _):
        def sub(n, _):
            root, stage = n // 3, n % 3
            g = t - root * OFFSET - STRIDE * stage

            @pl.when((g >= 0) & (g < UNITS) & jnp.logical_not(second_root & (root == 0)))
            def _():
                for axis in "xyz":
                    forward(axis, root, g // PIECES, g % PIECES, stage)

            return 0

        lax.fori_loop(0, 3 * ROOTS, sub, 0)

        def last(root, _):
            g = t - root * OFFSET - LATE

            @pl.when((g >= 0) & (g < UNITS) & jnp.logical_not(second_root & (root == 0)))
            def _():
                for index in range(PER):
                    receive(index, root, g // PIECES, g % PIECES)

            return 0

        lax.fori_loop(0, ROOTS, last, 0)
        return 0

    lax.fori_loop(0, UNITS + OFFSET + LATE, step, 0)

    for chunk in range(CHUNKS):

        @pl.when((me == 0) | (me > 3))
        def _():
            wait_tiles(PER, core_in.at[0, chunk])

        wait_tiles(PER, core_in.at[1, chunk])

    wait_tiles(2 * TILES, core_out.at[0])

    @pl.when(me < 4)
    def _():
        for chunk in range(CHUNKS):

            @pl.when((me != 0) | (chunk >= CHUNKS - WINDOW))
            def _():
                wait_tiles(PER, sent_root.at[chunk])

    for root in range(ROOTS):

        for n, axis in enumerate("xyz"):
            _, _, inside, line, inner, _, _, near = table[axis][root]
            sem = sent.at[root, n]
            straight = root == 0 and axis != "x"

            @pl.when(inside & line)
            def _():
                wait_tiles(CHUNKS * (9 if straight else 8), sem)

            @pl.when(inside & inner)
            def _():
                wait_tiles(CHUNKS * 3, sem)

            edge = inside & jnp.logical_not(line | inner)

            @pl.when(edge & jnp.logical_not(near))
            def _():
                wait_tiles(CHUNKS // 2 * 9, sem)

            if straight:

                @pl.when(edge & near)
                def _():
                    wait_tiles(CHUNKS // 2 * 7, sem)

    @pl.when(second_root)
    def _():
        panel_swap.wait_send()
        for chunk in range(CHUNKS):
            rhs_swap(chunk).wait_send()


def spread(rhs, panel, dinv):
    any_space = pl.BlockSpec(memory_space=pl.ANY)
    rhs, panel, dinv = (pltpu.with_memory_space_constraint(array, pltpu.HBM) for array in (rhs, panel, dinv))
    sem = pltpu.SemaphoreType.DMA
    return pl.pallas_call(
        spread_kernel,
        out_shape=pltpu.VMEM((4, TILES, NB, TW), jnp.bfloat16),
        in_specs=[any_space] * 3,
        out_specs=pl.BlockSpec(memory_space=pltpu.VMEM),
        scratch_shapes=[
            pltpu.VMEM((2, CHUNKS, NB, WIDTH), jnp.float32),
            pltpu.VMEM((2, NB, 4 * NB), jnp.bfloat16),
            pltpu.VMEM((2, NB, NB), jnp.float32),
            pltpu.VMEM((2, NB, 6 * NB), jnp.bfloat16),
            pltpu.VMEM((2, NB, 6 * NB), jnp.bfloat16),
            sem((2, CHUNKS + 1)),
            sem((CHUNKS + 1,)),
            sem((CHUNKS + 1,)),
            sem((ROOTS, TILES, PIECES)),
            sem((ROOTS, CHUNKS)),
            sem((1,)),
            sem((ROOTS, 3)),
            sem((CHUNKS,)),
        ],
        name="spread",
        compiler_params=pltpu.CompilerParams(
            collective_id=1, has_side_effects=True, vmem_limit_bytes=16 * 2**20
        ),
    )(rhs, panel, dinv)


BAND = 64
BANDS = 4 * NB // BAND
SLOTS = 4
WIDE = PER * TW
GROUPS = CHUNKS


def finish_kernel(buf, rhs, panel, sol, trail, stage, tstage, rhs_v, panel_v, load, out_s, out_t):
    me = lax.axis_index("row") * 8 + lax.axis_index("col")

    def rhs_copy(g):
        cols = pl.ds(g * WIDE, WIDE)
        return pltpu.make_async_copy(rhs.at[:, cols], rhs_v.at[:, cols], load.at[g])

    panel_copy = pltpu.make_async_copy(panel, panel_v, load.at[GROUPS])

    def sol_copy(band):
        rows = pl.ds(band * BAND, BAND)
        return pltpu.make_async_copy(stage.at[band % SLOTS], sol.at[rows], out_s.at[band % SLOTS])

    def trail_copy(g):
        return pltpu.make_async_copy(tstage.at[g % 2], trail.at[:, pl.ds(g * WIDE, WIDE)], out_t.at[g % 2])

    def widen(band):
        if band >= SLOTS:
            sol_copy(band - SLOTS).wait()
        block, first = band * BAND // NB, band * BAND % NB
        for tile in range(TILES):
            stage[band % SLOTS, :, tile * TW : (tile + 1) * TW] = buf[block, tile, first : first + BAND].astype(
                jnp.float32
            )
        sol_copy(band).start()

    def update(g):
        rhs_copy(g).wait()
        if g >= 2:
            trail_copy(g - 2).wait()
        low = [jnp.concatenate([buf[b, g * PER + i] for i in range(PER)], axis=1) for b in range(4)]
        tstage[g % 2] = rhs_v[:, g * WIDE : (g + 1) * WIDE] - dot(panel_v[...], jnp.concatenate(low, axis=0))
        trail_copy(g).start()

    panel_copy.start()
    for g in range(GROUPS):
        rhs_copy(g).start()
    each = BANDS // GROUPS
    for band in range(SLOTS):
        widen(band)
    panel_copy.wait()
    for block in range(4):
        cols = slice(block * NB, (block + 1) * NB)
        panel_v[:, cols] = jnp.where(me > block, panel_v[:, cols], jnp.zeros((NB, NB), jnp.bfloat16))
    for g in range(GROUPS):
        update(g)
        for band in range(SLOTS + g * each, min(SLOTS + (g + 1) * each, BANDS)):
            widen(band)
    for band in range(BANDS - SLOTS, BANDS):
        sol_copy(band).wait()
    for g in range(GROUPS - 2, GROUPS):
        trail_copy(g).wait()


def finish(buf, rhs, panel):
    any_space = pl.BlockSpec(memory_space=pl.ANY)
    buf = pltpu.with_memory_space_constraint(buf, pltpu.VMEM)
    return pl.pallas_call(
        finish_kernel,
        out_shape=(
            jax.ShapeDtypeStruct((4 * NB, TILES * TW), jnp.float32),
            jax.ShapeDtypeStruct((NB, TILES * TW), jnp.float32),
        ),
        in_specs=[pl.BlockSpec(memory_space=pltpu.VMEM), any_space, any_space],
        out_specs=(any_space, any_space),
        scratch_shapes=[
            pltpu.VMEM((SLOTS, BAND, TILES * TW), jnp.float32),
            pltpu.VMEM((2, NB, WIDE), jnp.float32),
            pltpu.VMEM((NB, TILES * TW), jnp.float32),
            pltpu.VMEM((NB, 4 * NB), jnp.bfloat16),
            pltpu.SemaphoreType.DMA((GROUPS + 1,)),
            pltpu.SemaphoreType.DMA((SLOTS,)),
            pltpu.SemaphoreType.DMA((2,)),
        ],
        name="finish",
        compiler_params=pltpu.CompilerParams(vmem_limit_bytes=24 * 2**20),
    )(buf, rhs, panel)


def body(rhs, panel, diag_inverse):
    own = rhs.reshape(rhs.shape[2], rhs.shape[3])
    factor = panel.reshape(panel.shape[2], panel.shape[3])
    tiles = spread(own, factor, diag_inverse)
    solved, trailing = finish(tiles, own, factor)
    return solved, trailing.reshape(rhs.shape)


def solution(mesh):
    in_specs = (P(None, ("row", "col"), None, None), P(None, ("row", "col"), None, None), P())
    out_specs = (P(), P(None, ("row", "col"), None, None))
    return jax.shard_map(body, mesh=mesh, in_specs=in_specs, out_specs=out_specs, check_vma=False)
```

```python
import jax
import jax.numpy as jnp
from jax import lax
from jax.experimental import pallas as pl
from jax.experimental.pallas import tpu as pltpu
from jax.sharding import PartitionSpec as P

MESH = pl.DeviceIdType.MESH
NB = 256
TW = 128
TILES = 32
PER = 8
SIDE = PER // 2
CHUNKS = TILES // PER
ROOTS = 2
WIDTH = SIDE * TW
PIECES = 2
ROWS = NB // PIECES
UNITS = CHUNKS * PIECES
STRIDE = 4
LATE = 14
OFFSET = 6
WINDOW = 1
KINDS = (("y", 2), ("z", 2), ("x", 0), ("y", 1), ("z", 1), ("x", 1), ("y", 3), ("z", 3))
PLANE = {"x": ("z", "y"), "y": ("x", "z"), "z": ("y", "x")}


def place():
    row, col = lax.axis_index("row"), lax.axis_index("col")
    return {"z": row // 4, "y": row % 4, "x": col // 2}, col % 2


def device(at, core):
    return (at["z"] * 4 + at["y"], at["x"] * 2 + core)


def moved(at, axis, by):
    new = dict(at)
    new[axis] = (at[axis] + by) % 4
    return new


def split(value):
    first = value.astype(jnp.bfloat16)
    rest = value - first.astype(jnp.float32)
    second = rest.astype(jnp.bfloat16)
    third = (rest - second.astype(jnp.float32)).astype(jnp.bfloat16)
    return first, second, third


def dot(left, right):
    return jnp.dot(left, right, preferred_element_type=jnp.float32)


def spread_kernel(
    rhs, panel, dinv, buf, rhs_v, panel_v, dinv_v, parts, mixed, local, swap_out, swap_in, got, core_in, core_out, sent, sent_root
):
    at, core = place()
    me = lax.axis_index("row") * 8 + lax.axis_index("col")
    sibling = device(at, 1 - core)
    first_root, second_root = me // 2 == 0, me // 2 == 1

    def spot(root, chunk, index):
        block = jnp.where(root == 0, core, 2 + index // SIDE)
        tile = chunk * PER + jnp.where(root == 0, index, core * SIDE + index % SIDE)
        return block, tile

    def send(block, tile, h, send_sem, recv_sem, to):
        piece = buf.at[block, tile, pl.ds(pl.multiple_of(h * ROWS, ROWS), ROWS)]
        pltpu.make_async_remote_copy(
            src_ref=piece,
            dst_ref=piece,
            send_sem=send_sem,
            recv_sem=recv_sem,
            device_id=to,
            device_id_type=MESH,
        ).start()

    def wait(ref, sem):
        pltpu.make_async_copy(ref, ref, sem).wait()

    def wait_tiles(count, sem):
        wait(buf.at[pl.ds(0, 2), pl.ds(0, count // 2)], sem)

    def take(root, chunk, index, h):
        wait(buf.at[0, 0, pl.ds(0, ROWS)], got.at[root, chunk * PER + index, h])

    def pass_over(root, chunk, index, h):
        block, tile = spot(root, chunk, index)
        send(block, tile, h, core_out.at[0], core_in.at[root, chunk], sibling)

    def pass_row(root, chunk, block, first, count):
        row = buf.at[block, pl.ds(first, count)]
        pltpu.make_async_remote_copy(
            src_ref=row,
            dst_ref=row,
            send_sem=core_out.at[0],
            recv_sem=core_in.at[root, chunk],
            device_id=sibling,
            device_id_type=MESH,
        ).start()

    def columns(half, chunk):
        return pl.ds(pl.multiple_of(chunk * 2 * WIDTH + half * WIDTH, WIDTH), WIDTH)

    def rhs_copy(half, chunk, slot):
        return pltpu.make_async_copy(rhs.at[:, columns(half, chunk)], rhs_v.at[slot, chunk], local.at[slot, chunk])

    def rhs_swap(chunk):
        return pltpu.make_async_remote_copy(
            src_ref=rhs.at[:, columns(1 - core, chunk)],
            dst_ref=rhs_v.at[core, chunk],
            send_sem=swap_out.at[chunk],
            recv_sem=swap_in.at[chunk],
            device_id=sibling,
            device_id_type=MESH,
        )

    panel_copy = pltpu.make_async_copy(panel, panel_v.at[core], local.at[0, CHUNKS])
    panel_swap = pltpu.make_async_remote_copy(
        src_ref=panel,
        dst_ref=panel_v.at[core],
        send_sem=swap_out.at[CHUNKS],
        recv_sem=swap_in.at[CHUNKS],
        device_id=sibling,
        device_id_type=MESH,
    )
    dinv_copy = pltpu.make_async_copy(dinv.at[pl.ds(2 * lax.rem(me // 2, 2), 2)], dinv_v, local.at[1, CHUNKS])

    peers = [(moved(at, axis, by), core) for axis in "xyz" for by in (1, 2, 3)]
    peers.append((at, 1 - core))
    barrier = pltpu.get_barrier_semaphore()
    for where, which in peers:
        pl.semaphore_signal(barrier, inc=1, device_id=device(where, which), device_id_type=MESH)
    at_second = {"x": jnp.int32(1), "y": jnp.int32(0), "z": jnp.int32(0)}
    relay = (at["x"] == 0) & ((at["y"] == 0) != (at["z"] == 0))

    @pl.when(second_root)
    def _():
        for axis in "yz":
            for j in (1, 2, 3):
                where = {"x": jnp.int32(0), "y": jnp.int32(0), "z": jnp.int32(0)}
                where[axis] = jnp.int32(j)
                pl.semaphore_signal(barrier, inc=1, device_id=device(where, core), device_id_type=MESH)

    def split_dinv():
        dinv_copy.wait()
        for i in range(2):
            one, two, three = split(dinv_v[i])
            for n, part in enumerate((one, one, one, two, two, three)):
                parts[i, :, n * NB : (n + 1) * NB] = part

    def product(i, work):
        one, two, three = split(work)
        right = jnp.concatenate([one, two, three, one, two, one], axis=0)
        return dot(parts[i], right)

    def mix(i, width):
        factor = panel_v[i, :, :width]
        exact = sum(dot(parts[i, :, n * NB : (n + 1) * NB], factor) for n in (0, 3, 5))
        one, two, _ = split(exact)
        mixed[i, :, :width] = one
        mixed[i, :, width : 2 * width] = two

    def solve(i, start, low):
        width = NB * len(low)
        return (start - dot(mixed[i, :, : 2 * width], jnp.concatenate(low + low, axis=0))).astype(jnp.bfloat16)

    def keep(block, tile, solved):
        for n in range(SIDE):
            buf[block, tile + n] = solved[:, n * TW : (n + 1) * TW]

    @pl.when(first_root)
    def _():
        dinv_copy.start()
        for chunk in range(CHUNKS):
            for half in range(2):
                rhs_copy(half, chunk, half).start()
        panel_copy.start()
        split_dinv()

    @pl.when(me == 0)
    def _():
        def one(chunk, _):
            for half in range(2):
                rhs_copy(half, chunk, half).wait()
                keep(0, chunk * PER + half * SIDE, product(0, rhs_v[half, chunk]).astype(jnp.bfloat16))
            return 0

        lax.fori_loop(0, CHUNKS, one, 0)
        panel_copy.wait()

    @pl.when(me == 1)
    def _():
        panel_copy.wait()
        mix(1, NB)

        def one(chunk, _):
            for half in range(2):
                rhs_copy(half, chunk, half).wait()
                rhs_v[half, chunk] = product(1, rhs_v[half, chunk])
            return 0

        lax.fori_loop(0, CHUNKS, one, 0)

    @pl.when(second_root)
    def _():
        dinv_copy.start()
        for chunk in range(CHUNKS):
            rhs_copy(core, chunk, core).start()
        panel_copy.start()
        split_dinv()

    pl.semaphore_wait(barrier, len(peers) + jnp.where(relay, 1, 0))

    @pl.when(second_root)
    def _():
        panel_swap.start()
        for chunk in range(CHUNKS):
            rhs_swap(chunk).start()

    def inject(root, chunk, index, h):
        axis, j = KINDS[index]
        if axis == "x":
            j = 2 - root + j
        block, tile = spot(root, chunk, index)
        to = device(moved(at, axis, j), core)
        send(block, tile, h, sent_root.at[chunk], got.at[root, chunk * PER + index, h], to)

    @pl.when(me == 0)
    def _():
        def one(chunk, _):
            @pl.when(chunk >= WINDOW)
            def _():
                wait_tiles(PER, sent_root.at[chunk - WINDOW])

            pass_row(0, chunk, 0, chunk * PER, PER)
            for h in range(PIECES):
                for index in range(PER):
                    inject(0, chunk, index, h)
            return 0

        lax.fori_loop(0, CHUNKS, one, 0)

    @pl.when(me == 1)
    def _():
        def one(chunk, _):
            wait_tiles(PER, core_in.at[0, chunk])
            for half in range(2):
                first = chunk * PER + half * SIDE
                low = jnp.concatenate([buf[0, first + n] for n in range(SIDE)], axis=1)
                keep(1, first, solve(1, rhs_v[half, chunk], [low]))
                for h in range(PIECES):
                    for n in range(SIDE):
                        inject(0, chunk, half * SIDE + n, h)
                pass_row(0, chunk, 1, first, SIDE)
            return 0

        lax.fori_loop(0, CHUNKS, one, 0)

    @pl.when(second_root)
    def _():
        panel_copy.wait()
        wait(panel_v.at[0], swap_in.at[CHUNKS])
        mix(0, 2 * NB)
        mix(1, 3 * NB)

        def start(chunk, _):
            rhs_copy(core, chunk, core).wait()
            wait(rhs_v.at[0, 0], swap_in.at[chunk])
            for i in range(2):
                rhs_v[i, chunk] = product(i, rhs_v[i, chunk])
            return 0

        lax.fori_loop(0, CHUNKS, start, 0)

        def one(chunk, _):
            for h in range(PIECES):
                for index in range(PER):
                    take(0, chunk, index, h)
                    pass_over(0, chunk, index, h)
            wait_tiles(PER, core_in.at[0, chunk])
            first = chunk * PER + core * SIDE
            low = [jnp.concatenate([buf[b, first + n] for n in range(SIDE)], axis=1) for b in range(2)]
            for i in range(2):
                solved = solve(i, rhs_v[i, chunk], low)
                low.append(solved)
                keep(2 + i, first, solved)
                for h in range(PIECES):
                    for n in range(SIDE):
                        inject(1, chunk, i * SIDE + n, h)
                pass_row(1, chunk, 2 + i, first, SIDE)
            return 0

        lax.fori_loop(0, CHUNKS, one, 0)

    def role(root, axis):
        rel = {"x": (at["x"] - root + 4) % 4, "y": at["y"], "z": at["z"]}
        one, two = (rel[name] for name in PLANE[axis])
        a = rel[axis]
        if axis == "x":
            index = jnp.where(a == 2 - root, 2, 5)
            inside = (a == 2 - root) | (a == 3 - root)
        else:
            index = jnp.where(a == 2, 0, jnp.where(a == 1, 3, 6)) + (1 if axis == "z" else 0)
            inside = a != 0
        line = (one == 0) & (two == 0)
        even = jnp.where(line, 0, jnp.where(two == 0, 1, 2))
        odd = jnp.where(line, 0, jnp.where(one == 0, 1, 2))
        none = jnp.int32(-1)
        even, odd = jnp.where(inside, even, none), jnp.where(inside, odd, none)
        near = (at["x"] == 1) & (rel["z" if axis == "y" else "y"] == 0) if root == 0 and axis != "x" else False
        return a, index, inside, line, (one != 0) & (two != 0), even, odd, near

    table = {axis: [role(root, axis) for root in range(ROOTS)] for axis in "xyz"}
    here = [(at["x"] == root) & (at["y"] == 0) & (at["z"] == 0) for root in range(ROOTS)]

    def forward(axis, root, chunk, h, stage):
        first = root == 0
        parity = chunk % 2 == 0
        pick = [jnp.where(first, p, q) for p, q in zip(table[axis][0][:2], table[axis][1][:2])]
        a, index = pick
        even, odd = (jnp.where(first, table[axis][0][n], table[axis][1][n]) for n in (5, 6))
        mine = jnp.where(parity, even, odd)
        near = first & table[axis][0][7]
        one, two = PLANE[axis]
        index_axis = "xyz".index(axis)

        @pl.when(mine == stage)
        def _():
            block, tile = spot(root, chunk, index)
            sem = sent.at[root, index_axis]
            arrived = got.at[root, chunk * PER + index, h]
            take(root, chunk, index, h)

            def along(p, q, by):
                p, q = device(moved(at, p, by), core), device(moved(at, q, by), core)
                return tuple(jnp.where(parity, i, j) for i, j in zip(p, q))

            if axis != "x":

                @pl.when((stage == 0) & first)
                def _():
                    send(block, tile, h, sem, arrived, device(at_second, core))

            @pl.when(stage == 0)
            def _():
                for by in (1, 3, 2):
                    send(block, tile, h, sem, arrived, along(one, two, by))

            @pl.when(stage <= 1)
            def _():
                for by in (1, 3, 2):
                    send(block, tile, h, sem, arrived, along(two, one, by))

            for by in (1, 3, 2):

                @pl.when(((stage != 0) & jnp.logical_not(near)) | ((a + by) % 4 != 0))
                def _():
                    send(block, tile, h, sem, arrived, device(moved(at, axis, by), core))

            pass_over(root, chunk, index, h)

    def receive(index, root, chunk, h):
        axis, j = KINDS[index]
        a = jnp.where(root == 0, table[axis][0][0], table[axis][1][0])
        if axis == "x":
            j = 2 - root + j
        at_root = jnp.where(root == 0, here[0], here[1])

        @pl.when((a != j) & jnp.logical_not(at_root))
        def _():
            take(root, chunk, index, h)
            pass_over(root, chunk, index, h)

    def step(t, _):
        def sub(n, _):
            root, stage = n // 3, n % 3
            g = t - root * OFFSET - STRIDE * stage

            @pl.when((g >= 0) & (g < UNITS) & jnp.logical_not(second_root & (root == 0)))
            def _():
                for axis in "xyz":
                    forward(axis, root, g // PIECES, g % PIECES, stage)

            return 0

        lax.fori_loop(0, 3 * ROOTS, sub, 0)

        def last(root, _):
            g = t - root * OFFSET - LATE

            @pl.when((g >= 0) & (g < UNITS) & jnp.logical_not(second_root & (root == 0)))
            def _():
                for index in range(PER):
                    receive(index, root, g // PIECES, g % PIECES)

            return 0

        lax.fori_loop(0, ROOTS, last, 0)
        return 0

    lax.fori_loop(0, UNITS + OFFSET + LATE, step, 0)

    for chunk in range(CHUNKS):

        @pl.when((me == 0) | (me > 3))
        def _():
            wait_tiles(PER, core_in.at[0, chunk])

        wait_tiles(PER, core_in.at[1, chunk])

    wait_tiles(2 * TILES, core_out.at[0])

    @pl.when(me < 4)
    def _():
        for chunk in range(CHUNKS):

            @pl.when((me != 0) | (chunk >= CHUNKS - WINDOW))
            def _():
                wait_tiles(PER, sent_root.at[chunk])

    for root in range(ROOTS):

        for n, axis in enumerate("xyz"):
            _, _, inside, line, inner, _, _, near = table[axis][root]
            sem = sent.at[root, n]
            straight = root == 0 and axis != "x"

            @pl.when(inside & line)
            def _():
                wait_tiles(CHUNKS * (9 if straight else 8), sem)

            @pl.when(inside & inner)
            def _():
                wait_tiles(CHUNKS * 3, sem)

            edge = inside & jnp.logical_not(line | inner)

            @pl.when(edge & jnp.logical_not(near))
            def _():
                wait_tiles(CHUNKS // 2 * 9, sem)

            if straight:

                @pl.when(edge & near)
                def _():
                    wait_tiles(CHUNKS // 2 * 7, sem)

    @pl.when(second_root)
    def _():
        panel_swap.wait_send()
        for chunk in range(CHUNKS):
            rhs_swap(chunk).wait_send()


def spread(rhs, panel, dinv):
    any_space = pl.BlockSpec(memory_space=pl.ANY)
    rhs, panel, dinv = (pltpu.with_memory_space_constraint(array, pltpu.HBM) for array in (rhs, panel, dinv))
    sem = pltpu.SemaphoreType.DMA
    return pl.pallas_call(
        spread_kernel,
        out_shape=pltpu.VMEM((4, TILES, NB, TW), jnp.bfloat16),
        in_specs=[any_space] * 3,
        out_specs=pl.BlockSpec(memory_space=pltpu.VMEM),
        scratch_shapes=[
            pltpu.VMEM((2, CHUNKS, NB, WIDTH), jnp.float32),
            pltpu.VMEM((2, NB, 4 * NB), jnp.bfloat16),
            pltpu.VMEM((2, NB, NB), jnp.float32),
            pltpu.VMEM((2, NB, 6 * NB), jnp.bfloat16),
            pltpu.VMEM((2, NB, 6 * NB), jnp.bfloat16),
            sem((2, CHUNKS + 1)),
            sem((CHUNKS + 1,)),
            sem((CHUNKS + 1,)),
            sem((ROOTS, TILES, PIECES)),
            sem((ROOTS, CHUNKS)),
            sem((1,)),
            sem((ROOTS, 3)),
            sem((CHUNKS,)),
        ],
        name="spread",
        compiler_params=pltpu.CompilerParams(
            collective_id=1, has_side_effects=True, vmem_limit_bytes=16 * 2**20
        ),
    )(rhs, panel, dinv)


BAND = 32
BANDS = 4 * NB // BAND
SLOTS = 12
WIDE = PER * TW
GROUPS = CHUNKS


def finish_kernel(buf, rhs, panel, sol, trail, stage, tstage, rhs_v, panel_v, load, out_s, out_t):
    me = lax.axis_index("row") * 8 + lax.axis_index("col")

    def rhs_copy(g):
        cols = pl.ds(g * WIDE, WIDE)
        return pltpu.make_async_copy(rhs.at[:, cols], rhs_v.at[:, cols], load.at[g])

    panel_copy = pltpu.make_async_copy(panel, panel_v, load.at[GROUPS])

    def sol_copy(band):
        rows = pl.ds(band * BAND, BAND)
        return pltpu.make_async_copy(stage.at[band % SLOTS], sol.at[rows], out_s.at[band % SLOTS])

    def trail_copy(g):
        return pltpu.make_async_copy(tstage.at[g % 2], trail.at[:, pl.ds(g * WIDE, WIDE)], out_t.at[g % 2])

    def widen(band):
        if band >= SLOTS:
            sol_copy(band - SLOTS).wait()
        block, first = band * BAND // NB, band * BAND % NB
        for tile in range(TILES):
            stage[band % SLOTS, :, tile * TW : (tile + 1) * TW] = buf[block, tile, first : first + BAND].astype(
                jnp.float32
            )
        sol_copy(band).start()

    def update(g):
        rhs_copy(g).wait()
        if g >= 2:
            trail_copy(g - 2).wait()
        low = [jnp.concatenate([buf[b, g * PER + i] for i in range(PER)], axis=1) for b in range(4)]
        tstage[g % 2] = rhs_v[:, g * WIDE : (g + 1) * WIDE] - dot(panel_v[...], jnp.concatenate(low, axis=0))
        trail_copy(g).start()

    panel_copy.start()
    for g in range(GROUPS):
        rhs_copy(g).start()
    each = BANDS // GROUPS
    for band in range(SLOTS):
        widen(band)
    panel_copy.wait()
    for block in range(4):
        cols = slice(block * NB, (block + 1) * NB)
        panel_v[:, cols] = jnp.where(me > block, panel_v[:, cols], jnp.zeros((NB, NB), jnp.bfloat16))
    for g in range(GROUPS):
        update(g)
        for band in range(SLOTS + g * each, min(SLOTS + (g + 1) * each, BANDS)):
            widen(band)
    for band in range(BANDS - SLOTS, BANDS):
        sol_copy(band).wait()
    for g in range(GROUPS - 2, GROUPS):
        trail_copy(g).wait()


def finish(buf, rhs, panel):
    any_space = pl.BlockSpec(memory_space=pl.ANY)
    buf = pltpu.with_memory_space_constraint(buf, pltpu.VMEM)
    return pl.pallas_call(
        finish_kernel,
        out_shape=(
            jax.ShapeDtypeStruct((4 * NB, TILES * TW), jnp.float32),
            jax.ShapeDtypeStruct((NB, TILES * TW), jnp.float32),
        ),
        in_specs=[pl.BlockSpec(memory_space=pltpu.VMEM), any_space, any_space],
        out_specs=(any_space, any_space),
        scratch_shapes=[
            pltpu.VMEM((SLOTS, BAND, TILES * TW), jnp.float32),
            pltpu.VMEM((2, NB, WIDE), jnp.float32),
            pltpu.VMEM((NB, TILES * TW), jnp.float32),
            pltpu.VMEM((NB, 4 * NB), jnp.bfloat16),
            pltpu.SemaphoreType.DMA((GROUPS + 1,)),
            pltpu.SemaphoreType.DMA((SLOTS,)),
            pltpu.SemaphoreType.DMA((2,)),
        ],
        name="finish",
        compiler_params=pltpu.CompilerParams(vmem_limit_bytes=24 * 2**20),
    )(buf, rhs, panel)


def body(rhs, panel, diag_inverse):
    own = rhs.reshape(rhs.shape[2], rhs.shape[3])
    factor = panel.reshape(panel.shape[2], panel.shape[3])
    tiles = spread(own, factor, diag_inverse)
    solved, trailing = finish(tiles, own, factor)
    return solved, trailing.reshape(rhs.shape)


def solution(mesh):
    in_specs = (P(None, ("row", "col"), None, None), P(None, ("row", "col"), None, None), P())
    out_specs = (P(), P(None, ("row", "col"), None, None))
    return jax.shard_map(body, mesh=mesh, in_specs=in_specs, out_specs=out_specs, check_vma=False)
```
